32 devices in a mesh: groups: 2 (over y), aux: 4 (over z), orb: 2 (over x), sub: 2 (over core).
Axes of the slice: x: 2, y: 2, z: 4, core: 2. Of those that a mesh axis runs over, the one named last changes fastest.
Arguments:
- three_index: bfloat16 [16, 32, 16, 128, 128], P(('groups', 'aux'), 'orb'), parts along dimension 0, may hold values from -0.125 to 0.125
- block_cols: int32 [8, 32, 16], P(('groups', 'aux'), 'orb'), parts along dimension 0, may hold values from 0 to 31, as said below
- live_count: int32 [8, 32], P(('groups', 'aux'), 'orb'), parts along dimension 0, may hold values from 1 to 16, as said below
- coefficients: bfloat16 [8192, 1024], P(('groups', 'orb'), 'sub'), parts along dimension 0, may hold values from -0.1875 to 0.1875
Outputs:
- exchange_matrix: float32 [8192, 4096], P(('groups', 'aux', 'sub'), 'orb'), parts along dimension 0
The draws below stay inside these ranges and needn't reach their ends.
There are 2 independent parts, one for each index of `groups`. The reference program is written for one: setup_inputs(seed, part) draws one part's arguments, and reference() takes and returns one part's arrays. A program takes and returns all parts, laid end to end along the dimension named above; each array names one. Nothing has to cross between parts.
Inputs may be any that keep to these rules, and one draw needn't show every extreme that they name: `block_cols`: within each row of 16 entries the basis blocks are distinct. Only the first live_count[a, m] slots of basis block m for aux block a hold screened blocks; the other slots are padding whose contents are not used. Some entry equals 16 in every draw.
All inputs are finite; a program needn't handle non-finite values.
Results may differ from the reference program's by a relative error of at most 0.0018.
Values may be sent and summed in bfloat16 or wider, within the bound.
No kernel may reach another device: no remote copies, remote signals or barrier semaphores. Data moves between devices by JAX's collectives and lax.ppermute only.
A program may use at most 128 MiB of HBM per device.

```python
import jax
import jax.numpy as jnp
from jax import lax

BASIS = 4096
OCC = 1024
BLOCK = 128
SLOTS = 16
AUX_DEV = 2
NB = 32
AUX = 8
ABLOCKS = 4


def draw_block_cols(key, part):
    key = jax.random.fold_in(key, 11)
    scores = jax.random.randint(key, (ABLOCKS, NB, NB), 0, 1 << 20) * NB + jnp.arange(NB, dtype=jnp.int32)[None, None, :]
    ordering = jnp.argsort(scores, axis=-1)
    return ordering[:, :, :SLOTS].astype(jnp.int32)


def draw_live_count(key, part):
    key = jax.random.fold_in(key, 23)
    first, second, third, fourth = jax.random.split(key, 4)
    base_level = 1 + jax.random.randint(first, (ABLOCKS, NB), 0, max(SLOTS // 3, 1))
    heavy_level = jax.random.randint(second, (ABLOCKS, NB), SLOTS // 2, SLOTS + 1)
    heavy_block = jax.random.randint(third, (), 0, ABLOCKS)
    top_column = jax.random.randint(fourth, (), 0, NB)
    block_ids = jnp.arange(ABLOCKS, dtype=jnp.int32)[:, None]
    basis_ids = jnp.arange(NB, dtype=jnp.int32)[None, :]
    counts = jnp.where(block_ids == heavy_block, heavy_level, base_level)
    counts = jnp.where((block_ids == heavy_block) & (basis_ids == top_column), SLOTS, counts)
    return counts.astype(jnp.int32)


def steps_of(key, shape, shards, smallest, high):
    def one(axis_at, blocks):
        draws = jax.random.uniform(jax.random.fold_in(jax.random.fold_in(key, 6), axis_at), (blocks,), jnp.float32, smallest / len(shards), high / len(shards))
        return jnp.repeat(jnp.exp(draws), shape[axis_at] // blocks).reshape((-1,) + (1,) * (len(shape) - axis_at - 1))

    level = one(*shards[0])
    for cut in shards[1:]:
        level = level * one(*cut)
    return level


def normal_values(stream_key, extent, width, bound, shards=(), kind=jnp.bfloat16):
    drawn = width * jax.random.normal(stream_key, extent, jnp.float32)
    if shards:
        drawn = drawn * steps_of(stream_key, extent, shards, -0.22, 0.18)
    return jnp.clip(drawn, -bound, bound).astype(kind)


def setup_inputs(seed: int = 0, part: int = 0) -> dict:
    arg_keys = jax.random.split(jax.random.key(seed), 5)
    own_keys = jax.random.split(jax.random.fold_in(arg_keys[4], part), 5)
    three_index = normal_values(own_keys[0], (AUX, NB, SLOTS, BLOCK, BLOCK), (BLOCK * SLOTS) ** -0.5, 0.125, ((0, 4), (1, 2)))
    block_cols = draw_block_cols(jax.random.fold_in(jax.random.fold_in(arg_keys[4], part), 71), part)
    live_count = draw_live_count(jax.random.fold_in(jax.random.fold_in(arg_keys[4], part), 71), part)
    coefficients = normal_values(own_keys[3], (BASIS, OCC), OCC ** -0.5, 0.1875, ((0, 2), (1, 2)))
    return dict(three_index=three_index, block_cols=block_cols, live_count=live_count, coefficients=coefficients)


def reference(three_index, block_cols, live_count, coefficients):
    coeff_blocks = coefficients.reshape(NB, BLOCK, OCC)
    slot_ids = jnp.arange(SLOTS, dtype=jnp.int32)

    def one_function(accumulated, aux_index):
        aux_block = (aux_index // AUX_DEV).astype(jnp.int32)
        columns = lax.dynamic_index_in_dim(block_cols, aux_block, 0, keepdims=False)
        counts = lax.dynamic_index_in_dim(live_count, aux_block, 0, keepdims=False)
        integrals = lax.dynamic_index_in_dim(three_index, aux_index, 0, keepdims=False)
        alive_mask = slot_ids[None, :] < counts[:, None]
        masked = jnp.where(alive_mask[:, :, None, None], integrals, jnp.zeros_like(integrals))
        picked = coeff_blocks[columns]
        transformed = jnp.einsum("msrc,msci->mri", masked.astype(jnp.float32), picked.astype(jnp.float32))
        transformed = transformed.reshape(BASIS, OCC).astype(jnp.bfloat16)
        return accumulated + jnp.dot(transformed, transformed.T, preferred_element_type=jnp.float32), None

    result, _ = lax.scan(one_function, jnp.zeros((BASIS, BASIS), jnp.float32), jnp.arange(AUX, dtype=jnp.int32))
    return result
```

```python
import functools

import jax
import jax.numpy as jnp
from jax import lax
from jax.experimental import pallas as pl
from jax.experimental.pallas import tpu as pltpu
from jax.sharding import PartitionSpec as P

GROUP = 4
VMEM_LIMIT = 40 * 1024 * 1024


def transform_kernel(columns, counts, x_ref, *refs, parts):
    coeff_refs = refs[:parts]
    out_ref, coeff_vmem, total, sems = refs[parts:]
    functions, together, slots, side, _ = x_ref.shape
    width = coeff_vmem.shape[1]

    @pl.when(pl.program_id(0) == 0)
    def _():
        copies = []
        for part, ref in enumerate(coeff_refs):
            rows = ref.shape[0]
            copy = pltpu.make_async_copy(ref, coeff_vmem.at[pl.ds(part * rows, rows)], sems.at[part])
            copy.start()
            copies.append(copy)
        for copy in copies:
            copy.wait()

    for inner in range(together):
        block = pl.program_id(0) * together + inner
        count = counts[block]

        def product(first, inner=inner, block=block, count=count):
            left = jnp.concatenate(
                [
                    jnp.concatenate([x_ref[p, inner, first + t] for t in range(GROUP)], axis=1)
                    for p in range(functions)
                ],
                axis=0,
            )
            lane = lax.broadcasted_iota(jnp.int32, left.shape, 1)
            left = jnp.where(lane < (count - first) * side, left, jnp.zeros_like(left))
            right = jnp.concatenate(
                [
                    coeff_vmem[pl.ds(pl.multiple_of(columns[block, first + t] * side, side), side), :]
                    for t in range(GROUP)
                ],
                axis=0,
            )
            return jnp.dot(left, right, preferred_element_type=jnp.float32)

        total[inner] = product(0)
        for first in range(GROUP, slots, GROUP):

            @pl.when(count > first)
            def _(first=first, inner=inner, product=product):
                total[inner] += product(first)

        for p in range(functions):
            out_ref[inner * side : (inner + 1) * side, p * width : (p + 1) * width] = total[
                inner, p * side : (p + 1) * side, :
            ].astype(out_ref.dtype)


def transform(three_index, columns, counts, coeff_parts):
    functions, blocks, slots, side, _ = three_index.shape
    part_rows, width = coeff_parts[0].shape
    parts = len(coeff_parts)
    together = next(t for t in (4, 2, 1) if blocks % t == 0)
    flops = 2 * functions * blocks * slots * side * side * width
    return pl.pallas_call(
        functools.partial(transform_kernel, parts=parts),
        grid_spec=pltpu.PrefetchScalarGridSpec(
            num_scalar_prefetch=2,
            grid=(blocks // together,),
            in_specs=[
                pl.BlockSpec((functions, together, slots, side, side), lambda m, *_: (0, m, 0, 0, 0))
            ]
            + [pl.BlockSpec(memory_space=pl.ANY)] * parts,
            out_specs=pl.BlockSpec((together * side, functions * width), lambda m, *_: (m, 0)),
            scratch_shapes=[
                pltpu.VMEM((parts * part_rows, width), jnp.bfloat16),
                pltpu.VMEM((together, functions * side, width), jnp.float32),
                pltpu.SemaphoreType.DMA((parts,)),
            ],
        ),
        out_shape=jax.ShapeDtypeStruct((blocks * side, functions * width), jnp.bfloat16),
        compiler_params=pltpu.CompilerParams(vmem_limit_bytes=VMEM_LIMIT),
        cost_estimate=pl.CostEstimate(flops=flops, bytes_accessed=three_index.size * 2, transcendentals=0),
    )(columns, counts, three_index, *coeff_parts)


def product_kernel(index, *refs, parts):
    out_ref = refs[-1]
    total = None
    for rows_ref, cols_ref in zip(refs[:parts], refs[parts:-1]):
        term = lax.dot_general(
            rows_ref[0], cols_ref[...], (((1,), (1,)), ((), ())), preferred_element_type=jnp.float32
        )
        total = term if total is None else total + term
    out_ref[...] = total


def row_product(index, rows, cols):
    parts = len(rows)
    height, depth = rows[0].shape[1:]
    length = cols[0].shape[0]
    tile = min(length, 512)
    return pl.pallas_call(
        functools.partial(product_kernel, parts=parts),
        grid_spec=pltpu.PrefetchScalarGridSpec(
            num_scalar_prefetch=1,
            grid=(length // tile,),
            in_specs=[pl.BlockSpec((1, height, depth), lambda c, index: (index[0], 0, 0))] * parts
            + [pl.BlockSpec((tile, depth), lambda c, index: (c, 0))] * parts,
            out_specs=pl.BlockSpec((height, tile), lambda c, index: (0, c)),
        ),
        out_shape=jax.ShapeDtypeStruct((height, length), jnp.float32),
        compiler_params=pltpu.CompilerParams(vmem_limit_bytes=VMEM_LIMIT),
        cost_estimate=pl.CostEstimate(
            flops=2 * height * length * depth * parts,
            bytes_accessed=parts * 2 * depth * (height + length) + 4 * height * length,
            transcendentals=0,
        ),
    )(index, *rows, *cols)


class Line:
    def __init__(self, aux, orb):
        self.aux, self.orb, self.owned = aux, orb, aux // orb

    def targets(self, phase, o):
        first = ((o + phase) % self.orb) * self.owned
        return list(range(first, first + self.owned))

    def chains(self, phase, o, direction):
        head = 0 if direction > 0 else self.aux - 1
        found = sorted((t for t in self.targets(phase, o) if t != head), key=lambda t: -t * direction)
        late = self.owned - len(found) if phase else 0
        return {t: place + late for place, t in enumerate(found)}

    def first_use(self, phase, o, z, target):
        if target == z:
            return 10 * self.aux
        direction = 1 if target > z else -1
        return self.chains(phase, o, direction)[target] + (z if direction > 0 else self.aux - 1 - z)

    def order(self, phase, o, z):
        return sorted(self.targets(phase, o), key=lambda d: (self.first_use(phase, o, z, d), d))

    def hop(self, phase, rank, step):
        pairs, position, final = [], {}, {}
        for o in range(self.orb):
            for direction in (1, -1):
                z = step if direction > 0 else self.aux - 1 - step
                for target, place in self.chains(phase, o, direction).items():
                    if place != rank or (target - z) * direction <= 0:
                        continue
                    pairs.append((z * self.orb + o, (z + direction) * self.orb + o))
                    position[z * self.orb + o] = self.order(phase, o, z).index(target)
                    if z + direction == target:
                        final[target * self.orb + o] = True
        return pairs, position, final


def lookup(table, place):
    return jnp.asarray(table, jnp.int32)[place]


def after(value, earlier):
    return value if earlier is None else lax.optimization_barrier((value, earlier))[0]


def shards(mesh, three_index, block_cols, live_count, coefficients):
    aux, orb, sub = mesh.shape["aux"], mesh.shape["orb"], mesh.shape["sub"]
    z, o, s = lax.axis_index("aux"), lax.axis_index("orb"), lax.axis_index("sub")
    place = z * orb + o
    line = Line(aux, orb)
    owned = line.owned
    blocks = three_index.shape[1]

    coeff_parts = [coefficients]
    for k in range(1, orb):
        coeff_parts.append(lax.ppermute(coefficients, "orb", [((t + k) % orb, t) for t in range(orb)]))
    all_blocks = blocks * orb
    columns = lax.rem(block_cols[0] - o * blocks + all_blocks, all_blocks)
    own = transform(three_index, columns, live_count[0], coeff_parts)
    length, depth = own.shape
    height = length // (owned * sub)
    chunks = max(1, height // 256)
    piece = height // chunks

    cols = [own]
    for t in range(1, sub):
        cols.append(lax.ppermute(own, "sub", [((u + t) % sub, u) for u in range(sub)]))
    views = [c.reshape(owned * sub, height, depth) for c in cols]

    came_rows, last = {}, None
    for k in range(1, orb):
        for q in range(owned):
            table = [line.order(k, (b - k) % orb, a)[q] % owned for a in range(aux) for b in range(orb)]
            mine = after(lookup(table, place), last)
            came_rows[k, q] = []
            for t in range(sub):
                sent = lax.dynamic_slice_in_dim(views[0], mine * sub + lax.rem(s - t + sub, sub), 1, 0)
                pairs = [
                    (((b + k) % orb) * sub + (c + t) % sub, b * sub + c) for b in range(orb) for c in range(sub)
                ]
                came_rows[k, q].append(lax.ppermute(sent, ("orb", "sub"), pairs))
                last = sent

    squares = jnp.sum(jnp.square(after(own, last).astype(jnp.float32)), axis=1)
    diagonal = jnp.sum(lax.all_gather(squares, ("aux", "sub")), axis=0)

    events = []
    for k in range(orb):
        base = owned * k - 1 if k else 0
        for q in range(owned):
            events.append((((base + q) * chunks - 0.5) if k or q else -1.0, 0, "product", k, q, 0, 0))
        finals = {c: [] for c in range(chunks)}
        for rank in range(owned):
            for step in range(aux - 1):
                pairs, _, final = line.hop(k, rank, step)
                if not pairs:
                    continue
                for c in range(chunks):
                    when = (base + rank) * chunks + c + step
                    events.append((when, step, "hop", k, rank, step, c))
                    if final:
                        finals[c].append((when + 1.5, rank, step))
        for c in range(chunks):
            events.append((max(f[0] for f in finals[c]), 0, "fold", k, c, [f[1:] for f in finals[c]], 0))
    events.sort(key=lambda e: e[:2])

    sums, came, result, last = {}, {}, None, squares
    for _, _, kind, k, a1, a2, c in events:
        if kind == "product":
            q = a1
            if k == 0:
                table = [line.order(k, b, a)[q] % owned for a in range(aux) for b in range(orb)]
                index = (lookup(table, place) * sub + s)[None]
                rows = views
            else:
                index = jnp.zeros((1,), jnp.int32)
                rows = came_rows[k, q]
            sums[k, q] = row_product(after(index, last), rows, cols)
            last = sums[k, q]
        elif kind == "hop":
            rank, step = a1, a2
            pairs, position, final = line.hop(k, rank, step)
            used = sorted(set(position.values()))
            arrived = came.get((k, rank, step - 1, c))
            if arrived is not None:
                arrived = after(arrived, last)
            value = sums[k, used[0]][c * piece : (c + 1) * piece]
            for q in used[1:]:
                flag = lookup([position.get(i) == q for i in range(aux * orb)], place)
                value = jnp.where(flag > 0, sums[k, q][c * piece : (c + 1) * piece], value)
            if arrived is not None:
                value = value + arrived.astype(jnp.float32)
            last = value.astype(jnp.bfloat16)
            came[k, rank, step, c] = lax.ppermute(last, ("aux", "orb"), pairs)
        else:
            at, terms = a1, a2
            if result is None:
                result = jnp.zeros((height, length), jnp.float32)
            flag = lookup([z_ in line.targets(k, o_) for z_ in range(aux) for o_ in range(orb)], place)
            rows = slice(at * piece, (at + 1) * piece)
            total = jnp.where(flag > 0, after(sums[k, owned - 1], last)[rows], 0.0)
            if k:
                total = total + result[rows]
            for rank, step in terms:
                final = line.hop(k, rank, step)[2]
                flag = lookup([i in final for i in range(aux * orb)], place)
                total = total + jnp.where(flag > 0, came[k, rank, step, at].astype(jnp.float32), 0.0)
            if k == orb - 1:
                start = lax.rem(z, owned) * sub * height + s * height + at * piece
                local = lax.div(z, owned) == o
                row = lax.broadcasted_iota(jnp.int32, total.shape, 0) + start
                col = lax.broadcasted_iota(jnp.int32, total.shape, 1)
                exact = lax.dynamic_slice_in_dim(diagonal, start, piece)
                total = jnp.where((row == col) & local, exact[:, None], total)
            result = lax.dynamic_update_slice(result, total, (at * piece, 0))
            last = result
    return result


def solution(mesh):
    return jax.shard_map(
        functools.partial(shards, mesh),
        mesh=mesh,
        in_specs=(
            P(("groups", "aux"), "orb", None, None, None),
            P(("groups", "aux"), "orb", None),
            P(("groups", "aux"), "orb"),
            P(("groups", "orb"), "sub"),
        ),
        out_specs=P(("groups", "aux", "sub"), "orb"),
        check_vma=False,
    )
```

```python
import functools

import jax
import jax.numpy as jnp
from jax import lax
from jax.experimental import pallas as pl
from jax.experimental.pallas import tpu as pltpu
from jax.sharding import PartitionSpec as P

GROUP = 4
VMEM_LIMIT = 40 * 1024 * 1024
COST = 1024


def transform_kernel(columns, counts, x_ref, *refs, parts):
    coeff_refs = refs[:parts]
    out_ref, coeff_vmem, total, sems = refs[parts:]
    functions, together, slots, side, _ = x_ref.shape
    width = coeff_vmem.shape[1]

    @pl.when(pl.program_id(0) == 0)
    def _():
        copies = []
        for part, ref in enumerate(coeff_refs):
            rows = ref.shape[0]
            copy = pltpu.make_async_copy(ref, coeff_vmem.at[pl.ds(part * rows, rows)], sems.at[part])
            copy.start()
            copies.append(copy)
        for copy in copies:
            copy.wait()

    for inner in range(together):
        block = pl.program_id(0) * together + inner
        count = counts[block]

        def product(first, inner=inner, block=block, count=count):
            left = jnp.concatenate(
                [
                    jnp.concatenate([x_ref[p, inner, first + t] for t in range(GROUP)], axis=1)
                    for p in range(functions)
                ],
                axis=0,
            )
            lane = lax.broadcasted_iota(jnp.int32, left.shape, 1)
            left = jnp.where(lane < (count - first) * side, left, jnp.zeros_like(left))
            right = jnp.concatenate(
                [
                    coeff_vmem[pl.ds(pl.multiple_of(columns[block, first + t] * side, side), side), :]
                    for t in range(GROUP)
                ],
                axis=0,
            )
            return jnp.dot(left, right, preferred_element_type=jnp.float32)

        total[inner] = product(0)
        for first in range(GROUP, slots, GROUP):

            @pl.when(count > first)
            def _(first=first, inner=inner, product=product):
                total[inner] += product(first)

        for p in range(functions):
            out_ref[inner * side : (inner + 1) * side, p * width : (p + 1) * width] = total[
                inner, p * side : (p + 1) * side, :
            ].astype(out_ref.dtype)


def transform(three_index, columns, counts, coeff_parts):
    functions, blocks, slots, side, _ = three_index.shape
    part_rows, width = coeff_parts[0].shape
    parts = len(coeff_parts)
    together = next(t for t in (4, 2, 1) if blocks % t == 0)
    return pl.pallas_call(
        functools.partial(transform_kernel, parts=parts),
        grid_spec=pltpu.PrefetchScalarGridSpec(
            num_scalar_prefetch=2,
            grid=(blocks // together,),
            in_specs=[
                pl.BlockSpec((functions, together, slots, side, side), lambda m, *_: (0, m, 0, 0, 0))
            ]
            + [pl.BlockSpec(memory_space=pl.ANY)] * parts,
            out_specs=pl.BlockSpec((together * side, functions * width), lambda m, *_: (m, 0)),
            scratch_shapes=[
                pltpu.VMEM((parts * part_rows, width), jnp.bfloat16),
                pltpu.VMEM((together, functions * side, width), jnp.float32),
                pltpu.SemaphoreType.DMA((parts,)),
            ],
        ),
        out_shape=jax.ShapeDtypeStruct((blocks * side, functions * width), jnp.bfloat16),
        compiler_params=pltpu.CompilerParams(vmem_limit_bytes=VMEM_LIMIT),
        cost_estimate=pl.CostEstimate(flops=COST, bytes_accessed=COST, transcendentals=0),
    )(columns, counts, three_index, *coeff_parts)


def product_kernel(index, *refs, parts, pieces):
    out_ref, piece_refs = refs[2 * parts], refs[2 * parts + 1 :]
    total = None
    for rows_ref, cols_ref in zip(refs[:parts], refs[parts : 2 * parts]):
        term = lax.dot_general(
            rows_ref[0], cols_ref[...], (((1,), (1,)), ((), ())), preferred_element_type=jnp.float32
        )
        total = term if total is None else total + term
    out_ref[...] = total
    for c, ref in enumerate(piece_refs):
        ref[...] = total[c * ref.shape[0] : (c + 1) * ref.shape[0]].astype(ref.dtype)


def row_product(index, rows, cols, pieces):
    parts = len(rows)
    height, depth = rows[0].shape[1:]
    length = cols[0].shape[0]
    tile = min(length, 512)
    return pl.pallas_call(
        functools.partial(product_kernel, parts=parts, pieces=pieces),
        grid_spec=pltpu.PrefetchScalarGridSpec(
            num_scalar_prefetch=1,
            grid=(length // tile,),
            in_specs=[
                pl.BlockSpec((1, height, depth), lambda c, index, t=t: (index[t], 0, 0)) for t in range(parts)
            ]
            + [pl.BlockSpec((tile, depth), lambda c, index: (c, 0))] * parts,
            out_specs=[pl.BlockSpec((height, tile), lambda c, index: (0, c))]
            + [pl.BlockSpec((height // pieces, tile), lambda c, index: (0, c))] * pieces,
        ),
        out_shape=[jax.ShapeDtypeStruct((height, length), jnp.float32)]
        + [jax.ShapeDtypeStruct((height // pieces, length), jnp.bfloat16)] * pieces,
        compiler_params=pltpu.CompilerParams(vmem_limit_bytes=VMEM_LIMIT),
        cost_estimate=pl.CostEstimate(flops=COST, bytes_accessed=COST, transcendentals=0),
    )(index, *rows, *cols)


class Line:
    def __init__(self, aux, orb):
        self.aux, self.orb, self.owned = aux, orb, aux // orb

    def targets(self, phase, o):
        first = ((o + phase) % self.orb) * self.owned
        return list(range(first, first + self.owned))

    def chains(self, phase, o, direction):
        head = 0 if direction > 0 else self.aux - 1
        found = sorted((t for t in self.targets(phase, o) if t != head), key=lambda t: -t * direction)
        late = self.owned - len(found) if phase else 0
        return {t: place + late for place, t in enumerate(found)}

    def first_use(self, phase, o, z, target):
        if target == z:
            return 10 * self.aux
        direction = 1 if target > z else -1
        return self.chains(phase, o, direction)[target] + (z if direction > 0 else self.aux - 1 - z)

    def order(self, phase, o, z):
        return sorted(self.targets(phase, o), key=lambda d: (self.first_use(phase, o, z, d), d))

    def hop(self, phase, rank, step):
        pairs, position, final = [], {}, {}
        for o in range(self.orb):
            for direction in (1, -1):
                z = step if direction > 0 else self.aux - 1 - step
                for target, place in self.chains(phase, o, direction).items():
                    if place != rank or (target - z) * direction <= 0:
                        continue
                    pairs.append((z * self.orb + o, (z + direction) * self.orb + o))
                    position[z * self.orb + o] = self.order(phase, o, z).index(target)
                    if z + direction == target:
                        final[target * self.orb + o] = True
        return pairs, position, final


def lookup(table, place):
    return jnp.asarray(table, jnp.int32)[place]


def after(value, earlier):
    return value if earlier is None else lax.optimization_barrier((value, earlier))[0]


def total_over(axis, size, value):
    if size & (size - 1):
        return lax.psum(value, axis)
    if size <= 4:
        return value + sum(
            lax.ppermute(value, axis, [(i, (i + shift) % size) for i in range(size)]) for shift in range(1, size)
        )
    shift = 1
    while shift < size:
        value = value + lax.ppermute(value, axis, [(i, (i + shift) % size) for i in range(size)])
        shift *= 2
    return value


def shards(mesh, three_index, block_cols, live_count, coefficients):
    aux, orb, sub = mesh.shape["aux"], mesh.shape["orb"], mesh.shape["sub"]
    z, o, s = lax.axis_index("aux"), lax.axis_index("orb"), lax.axis_index("sub")
    place = z * orb + o
    line = Line(aux, orb)
    owned = line.owned
    blocks = three_index.shape[1]

    coeff_parts = [coefficients]
    for k in range(1, orb):
        coeff_parts.append(lax.ppermute(coefficients, "orb", [((t + k) % orb, t) for t in range(orb)]))
    all_blocks = blocks * orb
    columns = lax.rem(block_cols[0] - o * blocks + all_blocks, all_blocks)
    own = transform(three_index, columns, live_count[0], coeff_parts)
    length, depth = own.shape
    height = length // (owned * sub)
    pieces = [1] + [max(1, height // 256)] * (orb - 1)
    beats = pieces[-1]

    cols = [own]
    for t in range(1, sub):
        cols.append(lax.ppermute(own, "sub", [((u + t) % sub, u) for u in range(sub)]))
    views = [c.reshape(owned * sub, height, depth) for c in cols]
    halves = total_over("aux", aux, jnp.sum(jnp.square(own.astype(jnp.float32)), axis=1))
    diagonal = total_over("sub", sub, halves)

    came_rows = {}
    for k in range(1, orb):
        for q in range(owned):
            table = [line.order(k, (b - k) % orb, a)[q] % owned for a in range(aux) for b in range(orb)]
            block = lookup(table, place) * sub + s
            message = jnp.concatenate([lax.dynamic_slice_in_dim(view, block, 1, 0) for view in views])
            pairs = [((b + k) % orb, b) for b in range(orb)]
            came_rows[k, q] = lax.ppermute(message, "orb", pairs)

    events = []
    for k in range(orb):
        base = (owned * k - 1 if k else 0) * beats
        wide = beats // pieces[k]
        ready = [base + q * beats - 0.5 if k else 0.25 * q - 1 for q in range(owned)]
        for q in range(owned):
            events.append((ready[q], 0, "product", k, q, 0, 0))
        finals = {c: [] for c in range(pieces[k])}
        for rank in range(owned):
            for step in range(aux - 1):
                pairs, _, final = line.hop(k, rank, step)
                if not pairs:
                    continue
                for c in range(pieces[k]):
                    when = base + rank * beats + (c + step) * wide
                    events.append((when if step else ready[rank] + 0.1, step, "hop", k, rank, step, c))
                    if final:
                        finals[c].append((when + wide + 0.5, rank, step))
        for c in range(pieces[k]):
            events.append((max(f[0] for f in finals[c]), 0, "fold", k, c, [f[1:] for f in finals[c]], 0))
    events.sort(key=lambda e: e[:2])

    sums, heads, came, result, last = {}, {}, {}, None, halves
    for _, _, kind, k, a1, a2, c in events:
        piece = height // pieces[k]
        if kind == "product":
            q = a1
            if k == 0:
                table = [line.order(k, b, a)[q] % owned for a in range(aux) for b in range(orb)]
                index = jnp.broadcast_to(lookup(table, place) * sub + s, (sub,))
                rows = views
            else:
                index = jnp.arange(sub, dtype=jnp.int32)
                rows = [came_rows[k, q]] * sub
            sums[k, q], *heads[k, q] = row_product(after(index, last), rows, cols, pieces[k])
            last = sums[k, q]
        elif kind == "hop":
            rank, step = a1, a2
            pairs, position, final = line.hop(k, rank, step)
            used = sorted(set(position.values()))
            if step == 0 and len(used) == 1:
                value = heads[k, used[0]][c]
            else:
                value = sums[k, used[0]][c * piece : (c + 1) * piece]
                for q in used[1:]:
                    flag = lookup([position.get(i) == q for i in range(aux * orb)], place)
                    value = jnp.where(flag > 0, sums[k, q][c * piece : (c + 1) * piece], value)
                if step:
                    value = value + after(came[k, rank, step - 1, c], last).astype(jnp.float32)
                value = value.astype(jnp.bfloat16)
                last = value
            came[k, rank, step, c] = lax.ppermute(value, ("aux", "orb"), pairs)
        else:
            at, terms = a1, a2
            flag = lookup([z_ in line.targets(k, o_) for z_ in range(aux) for o_ in range(orb)], place)
            rows = slice(at * piece, (at + 1) * piece)
            total = jnp.where(flag > 0, after(sums[k, owned - 1], last)[rows], 0.0)
            for rank, step in terms:
                final = line.hop(k, rank, step)[2]
                flag = lookup([i in final for i in range(aux * orb)], place)
                total = total + jnp.where(flag > 0, came[k, rank, step, at].astype(jnp.float32), 0.0)
            if k == 0:
                start = lax.rem(z, owned) * sub * height + s * height
                local = lax.div(z, owned) == o
                row = lax.broadcasted_iota(jnp.int32, total.shape, 0) + start
                col = lax.broadcasted_iota(jnp.int32, total.shape, 1)
                exact = lax.dynamic_slice_in_dim(diagonal, start, height)
                total = jnp.where((row == col) & local, exact[:, None], total)
                result = total
            else:
                result = lax.dynamic_update_slice(result, result[rows] + total, (at * piece, 0))
            last = result
    return result


def solution(mesh):
    return jax.shard_map(
        functools.partial(shards, mesh),
        mesh=mesh,
        in_specs=(
            P(("groups", "aux"), "orb", None, None, None),
            P(("groups", "aux"), "orb", None),
            P(("groups", "aux"), "orb"),
            P(("groups", "orb"), "sub"),
        ),
        out_specs=P(("groups", "aux", "sub"), "orb"),
        check_vma=False,
    )
```

```python
import functools

import jax
import jax.numpy as jnp
from jax import lax
from jax.experimental import pallas as pl
from jax.experimental.pallas import tpu as pltpu
from jax.sharding import PartitionSpec as P

GROUP = 4
VMEM_LIMIT = 40 * 1024 * 1024
COST = 1024
EXTRA = 16


def transform_kernel(order, columns, bounds, x_ref, *refs, parts, last, together):
    coeff_refs, refs = refs[:parts], refs[parts:]
    if last:
        early_ref, out_ref, x_vmem, coeff_vmem, total, sems, x_sems = refs
    else:
        out_ref, x_vmem, coeff_vmem, total, sems, x_sems = refs
    functions, blocks, slots, side, _ = x_ref.shape
    width = coeff_vmem.shape[1]
    top = coeff_vmem.shape[0] // side - 1

    def x_copy(block, i):
        return pltpu.make_async_copy(
            x_ref.at[:, block, order[block, i]], x_vmem.at[block, i], x_sems.at[block, i]
        )

    @pl.when(pl.program_id(0) == 0)
    def _():
        copies, done = [], 0
        for part, ref in enumerate(coeff_refs):
            rows = ref.shape[0]
            copy = pltpu.make_async_copy(ref, coeff_vmem.at[pl.ds(done, rows)], sems.at[part])
            copy.start()
            copies.append(copy)
            done += rows

        @pl.loop(0, blocks)
        def _(block):
            @pl.loop(bounds[block, 0], bounds[block, 1])
            def _(i):
                x_copy(block, i).start()

        for copy in copies:
            copy.wait()

    @pl.loop(0, together)
    def _(inner):
        block = pl.program_id(0) * together + inner
        start = bounds[block, 0]
        count = bounds[block, 1] - start

        @pl.loop(start, bounds[block, 1])
        def _(i):
            x_copy(block, i).wait()

        def product(first, group, masked):
            slot = [jnp.minimum(start + first + t, slots - 1) for t in range(group)]
            left = jnp.concatenate(
                [jnp.concatenate([x_vmem[block, i, p] for i in slot], axis=1) for p in range(functions)],
                axis=0,
            )
            if masked:
                lane = lax.broadcasted_iota(jnp.int32, left.shape, 1)
                left = jnp.where(lane < (count - first) * side, left, jnp.zeros_like(left))
            right = jnp.concatenate(
                [
                    coeff_vmem[pl.ds(pl.multiple_of(jnp.minimum(columns[block, i], top) * side, side), side), :]
                    for i in slot
                ],
                axis=0,
            )
            return jnp.dot(left, right, preferred_element_type=jnp.float32)

        total[...] = early_ref[inner] if last else jnp.zeros_like(total)
        full = lax.div(count, GROUP)
        rest = count - full * GROUP

        @pl.loop(0, full)
        def _(g):
            total[...] += product(g * GROUP, GROUP, False)

        @pl.when(rest > GROUP // 2)
        def _():
            total[...] += product(full * GROUP, GROUP, True)

        @pl.when((rest > 0) & (rest <= GROUP // 2))
        def _():
            total[...] += product(full * GROUP, GROUP // 2, True)

        if last:
            rows = pl.ds(pl.multiple_of(inner * side, side), side)
            for p in range(functions):
                out_ref[rows, p * width : (p + 1) * width] = total[p * side : (p + 1) * side, :].astype(
                    out_ref.dtype
                )
        else:
            out_ref[inner] = total[...]


def transform(three_index, order, columns, bounds, coeff_parts, early=None):
    functions, blocks, slots, side, _ = three_index.shape
    width = coeff_parts[0].shape[1]
    parts = len(coeff_parts)
    together = next(t for t in (2, 1) if blocks % t == 0)
    sums = pl.BlockSpec((together, functions * side, width), lambda m, *_: (m, 0, 0))
    last = early is not None
    return pl.pallas_call(
        functools.partial(transform_kernel, parts=parts, last=last, together=together),
        grid_spec=pltpu.PrefetchScalarGridSpec(
            num_scalar_prefetch=3,
            grid=(blocks // together,),
            in_specs=[pl.BlockSpec(memory_space=pl.ANY)] * (parts + 1) + [sums] * last,
            out_specs=pl.BlockSpec((together * side, functions * width), lambda m, *_: (m, 0)) if last else sums,
            scratch_shapes=[
                pltpu.VMEM((blocks, slots, functions, side, side), jnp.bfloat16),
                pltpu.VMEM((sum(c.shape[0] for c in coeff_parts), width), jnp.bfloat16),
                pltpu.VMEM((functions * side, width), jnp.float32),
                pltpu.SemaphoreType.DMA((parts,)),
                pltpu.SemaphoreType.DMA((blocks, slots)),
            ],
        ),
        out_shape=jax.ShapeDtypeStruct((blocks * side, functions * width), jnp.bfloat16)
        if last
        else jax.ShapeDtypeStruct((blocks, functions * side, width), jnp.float32),
        compiler_params=pltpu.CompilerParams(vmem_limit_bytes=VMEM_LIMIT),
        cost_estimate=pl.CostEstimate(flops=COST, bytes_accessed=COST, transcendentals=0),
    )(order, columns, bounds, three_index, *coeff_parts, *([early] * last))


def collect_kernel(index, *refs, parts):
    view_refs, out_refs, sems = refs[:parts], refs[parts:-1], refs[-1]
    copies = []
    for q, out_ref in enumerate(out_refs):
        for t, ref in enumerate(view_refs):
            copies.append(pltpu.make_async_copy(ref.at[index[q]], out_ref.at[t], sems.at[q, t]))
            copies[-1].start()
    for copy in copies:
        copy.wait()


def collect(index, views, count):
    parts = len(views)
    shape = (parts,) + views[0].shape[1:]
    return pl.pallas_call(
        functools.partial(collect_kernel, parts=parts),
        grid_spec=pltpu.PrefetchScalarGridSpec(
            num_scalar_prefetch=1,
            grid=(1,),
            in_specs=[pl.BlockSpec(memory_space=pl.ANY)] * parts,
            out_specs=[pl.BlockSpec(memory_space=pl.ANY)] * count,
            scratch_shapes=[pltpu.SemaphoreType.DMA((count, parts))],
        ),
        out_shape=[jax.ShapeDtypeStruct(shape, views[0].dtype)] * count,
        cost_estimate=pl.CostEstimate(flops=COST, bytes_accessed=COST, transcendentals=0),
    )(index, *views)


def store_rounded(out_ref, total, first_diagonal, carried):
    rows, tile = total.shape
    rounded = total.astype(out_ref.dtype)
    out_ref[:rows] = rounded
    if out_ref.shape[0] == rows:
        return
    row = lax.broadcasted_iota(jnp.int32, total.shape, 0) + first_diagonal
    col = lax.broadcasted_iota(jnp.int32, total.shape, 1) + pl.program_id(0) * tile
    lost = jnp.where(row == col, total - rounded.astype(jnp.float32), 0.0)
    lost = jnp.sum(lost, axis=0, keepdims=True)
    if carried is not None:
        lost = lost + carried
    extra = lax.broadcasted_iota(jnp.int32, (EXTRA, tile), 0)
    out_ref[rows:] = jnp.where(extra == 0, lost, 0.0).astype(out_ref.dtype)


def forward_kernel(index, sums_ref, came_ref, out_ref, *, first):
    rows = sums_ref.shape[0]
    total = sums_ref[...] + came_ref[:rows].astype(jnp.float32)
    carried = came_ref[rows : rows + 1].astype(jnp.float32)
    store_rounded(out_ref, total, index[0] + first, carried)


def forward(index, sums, came, piece, c):
    length = sums.shape[1]
    tile = min(length, 1024)
    return pl.pallas_call(
        functools.partial(forward_kernel, first=c * piece),
        grid_spec=pltpu.PrefetchScalarGridSpec(
            num_scalar_prefetch=1,
            grid=(length // tile,),
            in_specs=[
                pl.BlockSpec((piece, tile), lambda j, index: (c, j)),
                pl.BlockSpec((piece + EXTRA, tile), lambda j, index: (0, j)),
            ],
            out_specs=pl.BlockSpec((piece + EXTRA, tile), lambda j, index: (0, j)),
        ),
        out_shape=jax.ShapeDtypeStruct(came.shape, came.dtype),
        compiler_params=pltpu.CompilerParams(vmem_limit_bytes=VMEM_LIMIT),
        cost_estimate=pl.CostEstimate(flops=COST, bytes_accessed=COST, transcendentals=0),
    )(index, sums, came)


def product_kernel(index, *refs, parts, extra):
    out_ref, piece_refs = refs[2 * parts], refs[2 * parts + 1 :]
    total = None
    for rows_ref, cols_ref in zip(refs[:parts], refs[parts : 2 * parts]):
        term = lax.dot_general(
            rows_ref[0], cols_ref[...], (((1,), (1,)), ((), ())), preferred_element_type=jnp.float32
        )
        total = term if total is None else total + term
    out_ref[...] = total
    for c, ref in enumerate(piece_refs):
        rows = ref.shape[0] - extra
        store_rounded(ref, total[c * rows : (c + 1) * rows], index[0] * total.shape[0] + c * rows, None)


def row_product(index, rows, cols, pieces, extra):
    parts = len(rows)
    height, depth = rows[0].shape[1:]
    length = cols[0].shape[0]
    tile = min(length, 512)
    taller = height // max(pieces, 1) + extra
    return pl.pallas_call(
        functools.partial(product_kernel, parts=parts, extra=extra),
        grid_spec=pltpu.PrefetchScalarGridSpec(
            num_scalar_prefetch=1,
            grid=(length // tile,),
            in_specs=[
                pl.BlockSpec((1, height, depth), lambda c, index, t=t: (index[t], 0, 0)) for t in range(parts)
            ]
            + [pl.BlockSpec((tile, depth), lambda c, index: (c, 0))] * parts,
            out_specs=[pl.BlockSpec((height, tile), lambda c, index: (0, c))]
            + [pl.BlockSpec((taller, tile), lambda c, index: (0, c))] * pieces,
        ),
        out_shape=[jax.ShapeDtypeStruct((height, length), jnp.float32)]
        + [jax.ShapeDtypeStruct((taller, length), jnp.bfloat16)] * pieces,
        compiler_params=pltpu.CompilerParams(vmem_limit_bytes=VMEM_LIMIT),
        cost_estimate=pl.CostEstimate(flops=COST, bytes_accessed=COST, transcendentals=0),
    )(index, *rows, *cols)


class Line:
    def __init__(self, aux, orb):
        self.aux, self.orb, self.owned = aux, orb, aux // orb

    def targets(self, phase, o):
        first = ((o + phase) % self.orb) * self.owned
        return list(range(first, first + self.owned))

    def chains(self, phase, o, direction):
        head = 0 if direction > 0 else self.aux - 1
        found = sorted((t for t in self.targets(phase, o) if t != head), key=lambda t: -t * direction)
        late = self.owned - len(found) if phase else 0
        return {t: place + late for place, t in enumerate(found)}

    def first_use(self, phase, o, z, target):
        if target == z:
            return 10 * self.aux
        direction = 1 if target > z else -1
        return self.chains(phase, o, direction)[target] + (z if direction > 0 else self.aux - 1 - z)

    def order(self, phase, o, z):
        return sorted(self.targets(phase, o), key=lambda d: (self.first_use(phase, o, z, d), d))

    def hop(self, phase, rank, step):
        pairs, position, final = [], {}, {}
        for o in range(self.orb):
            for direction in (1, -1):
                z = step if direction > 0 else self.aux - 1 - step
                for target, place in self.chains(phase, o, direction).items():
                    if place != rank or (target - z) * direction <= 0:
                        continue
                    pairs.append((z * self.orb + o, (z + direction) * self.orb + o))
                    position[z * self.orb + o] = self.order(phase, o, z).index(target)
                    if z + direction == target:
                        final[target * self.orb + o] = True
        return pairs, position, final


def lookup(table, place):
    return jnp.asarray(table, jnp.int32)[place]


def after(value, earlier):
    return value if earlier is None else lax.optimization_barrier((value, earlier))[0]


def shards(mesh, three_index, block_cols, live_count, coefficients):
    aux, orb, sub = mesh.shape["aux"], mesh.shape["orb"], mesh.shape["sub"]
    z, o, s = lax.axis_index("aux"), lax.axis_index("orb"), lax.axis_index("sub")
    place = z * orb + o
    line = Line(aux, orb)
    owned = line.owned
    blocks = three_index.shape[1]

    side = three_index.shape[3]
    share = blocks // 3 if aux % 2 == 0 else 0
    parity = lax.rem(z, 2)
    firsts, rests = [], []
    for k in range(1, orb):
        pairs = [((t + k) % orb, t) for t in range(orb)]
        if share:
            first = lax.dynamic_slice_in_dim(coefficients, parity * share * side, share * side)
            firsts.append(lax.ppermute(first, "orb", pairs))
        rests.append(lax.ppermute(coefficients[2 * share * side :], "orb", pairs))

    slots = three_index.shape[2]
    all_blocks = blocks * orb
    columns = lax.rem(block_cols[0] - o * blocks + all_blocks, all_blocks)
    slot = lax.broadcasted_iota(jnp.int32, columns.shape, 1)
    alive = slot < live_count[0][:, None]
    mine = columns < blocks
    rank_key = jnp.where(alive, jnp.where(mine, 0, slots), 2 * slots) + slot
    rank = jnp.sum((rank_key[:, None, :] < rank_key[:, :, None]).astype(jnp.int32), axis=2)
    within = lax.rem(columns, blocks)
    half = lax.div(within, max(share, 1))
    moved = jnp.where(
        within >= 2 * share,
        within - share,
        jnp.where(half == parity, within - half * share, within - half * share + blocks - share),
    )
    placed = jnp.where(mine, columns, columns - within - blocks + moved)
    at_rank = rank[:, None, :] == lax.broadcasted_iota(jnp.int32, (1, slots, 1), 1)
    order = jnp.sum(jnp.where(at_rank, slot[:, None, :], 0), axis=2)
    columns = jnp.sum(jnp.where(at_rank, placed[:, None, :], 0), axis=2)
    live = jnp.sum(alive.astype(jnp.int32), axis=1)
    near = jnp.sum((alive & mine).astype(jnp.int32), axis=1)
    bounds = jnp.stack([jnp.zeros_like(near), near], axis=1)
    early = transform(three_index, order, columns, bounds, [coefficients])
    coeff_parts = []
    for k in range(1, orb):
        if not share:
            coeff_parts.append(rests[k - 1])
            continue
        handed = lax.ppermute(after(firsts[k - 1], early), "aux", [(i, i ^ 1) for i in range(aux)])
        coeff_parts += [firsts[k - 1], rests[k - 1], handed]
    if coeff_parts:
        bounds = jnp.stack([near, live], axis=1)
        own = transform(three_index, order, columns, bounds, coeff_parts, early)
    else:
        functions, width = three_index.shape[0], coefficients.shape[1]
        own = early.reshape(blocks, functions, side, width).transpose(0, 2, 1, 3)
        own = own.reshape(blocks * side, functions * width).astype(jnp.bfloat16)
    length, depth = own.shape
    height = length // (owned * sub)
    halves = 2 if height % 256 == 0 else 1

    def pieces(k, rank):
        return 2 * halves if k == orb - 1 and rank == owned - 1 and k else halves

    cols = [own]
    for t in range(1, sub):
        cols.append(lax.ppermute(own, "sub", [((u + t) % sub, u) for u in range(sub)]))
    views = [c.reshape(owned * sub, height, depth) for c in cols]

    blocks_sent = []
    for k in range(1, orb):
        for q in range(owned):
            table = [line.order(k, (b - k) % orb, a)[q] % owned for a in range(aux) for b in range(orb)]
            blocks_sent.append(lookup(table, place) * sub + s)
    came_rows = {}
    if blocks_sent:
        messages = collect(jnp.stack(blocks_sent), views, len(blocks_sent))
        for k in range(1, orb):
            for q in range(owned):
                pairs = [((b + k) % orb, b) for b in range(orb)]
                came_rows[k, q] = lax.ppermute(messages[(k - 1) * owned + q], "orb", pairs)
    own_blocks = [
        lookup([line.order(0, b, a)[q] % owned for a in range(aux) for b in range(orb)], place) * sub + s
        for q in range(owned)
    ]

    events, finals = [], []
    for k in range(orb):
        base = (owned * k - 1 if k else 0) * halves
        ready = [base + q * halves - 0.4 if k else 0.25 * q - 1 for q in range(owned)]
        for q in range(owned):
            events.append((ready[q], 0, "product", k, q, 0, 0))
        arrivals = [0]
        for rank in range(owned):
            wide = halves / pieces(k, rank)
            for step in range(aux - 1):
                pairs, _, final = line.hop(k, rank, step)
                if not pairs:
                    continue
                for c in range(pieces(k, rank)):
                    when = base + rank * halves + (c + step) * wide
                    events.append((when if step or c else ready[rank] + 0.1, step, "hop", k, rank, step, c))
                    arrivals.append(when + wide)
                if final:
                    finals.append((k, rank, step))
        if k < orb - 1:
            for c in range(halves):
                events.append((max(arrivals) + 0.6, 0, "fold", k, c, halves, 0))
        else:
            count = max(pieces(k, rank) for rank in range(owned))
            for c in range(count):
                late = max(arrivals) - (count - 1 - c) * halves / count
                events.append((late + 0.6, 0, "fold", k, c, count, 0))
    events.sort(key=lambda e: e[:2])

    sums, heads, came, result, last = {}, {}, {}, None, None
    for _, _, kind, k, a1, a2, c in events:
        extra = 0 if k else EXTRA
        if kind == "product":
            q = a1
            if k == 0:
                index = jnp.broadcast_to(own_blocks[q], (sub,))
                rows = views
            else:
                index = jnp.arange(sub, dtype=jnp.int32)
                rows = [came_rows[k, q]] * sub
            sums[k, q], *heads[k, q] = row_product(after(index, last), rows, cols, halves, extra)
            last = sums[k, q]
        elif kind == "hop":
            rank, step = a1, a2
            pairs, position, final = line.hop(k, rank, step)
            used = sorted(set(position.values()))
            flags = [lookup([position.get(i) == q for i in range(aux * orb)], place) for q in used]
            piece = height // pieces(k, rank)
            if step == 0 and len(used) == 1 and pieces(k, rank) == halves:
                value = heads[k, used[0]][c]
                value = after(value, last) if c else value
            elif k == 0:
                index, value = own_blocks[used[0]], sums[k, used[0]]
                head = heads[k, used[0]][c]
                for q, flag in zip(used[1:], flags[1:]):
                    index = jnp.where(flag > 0, own_blocks[q], index)
                    if step:
                        value = jnp.where(flag > 0, sums[k, q], value)
                    else:
                        head = jnp.where(flag > 0, heads[k, q][c], head)
                if step:
                    index = after((index * height)[None], last)
                    value = forward(index, value, came[k, rank, step - 1, c], piece, c)
                else:
                    value = after(head, last)
                last = value
            else:
                value = sums[k, used[0]] if step else after(sums[k, used[0]], last)
                value = value[c * piece : (c + 1) * piece]
                for q, flag in zip(used[1:], flags[1:]):
                    value = jnp.where(flag > 0, sums[k, q][c * piece : (c + 1) * piece], value)
                if step:
                    value = value + after(came[k, rank, step - 1, c], last).astype(jnp.float32)
                value = value.astype(jnp.bfloat16)
                last = value
            came[k, rank, step, c] = lax.ppermute(value, ("aux", "orb"), pairs)
        else:
            at, count = a1, a2
            piece = height // count
            rows = slice(at * piece, (at + 1) * piece)
            flag = lookup([z_ in line.targets(k, o_) for z_ in range(aux) for o_ in range(orb)], place)
            total = jnp.where(flag > 0, after(sums[k, owned - 1], last)[rows], 0.0)
            for k_, rank, step in finals:
                if k_ != k:
                    continue
                final = line.hop(k, rank, step)[2]
                flag = lookup([i in final for i in range(aux * orb)], place)
                sent = height // pieces(k, rank)
                first = at * piece % sent
                message = came[k, rank, step, at * piece // sent]
                term = message[first : first + piece].astype(jnp.float32)
                if extra:
                    start = (lax.rem(z, owned) * sub + s) * height + at * piece
                    row = lax.broadcasted_iota(jnp.int32, total.shape, 0) + start
                    col = lax.broadcasted_iota(jnp.int32, total.shape, 1)
                    term = term + jnp.where(row == col, message[sent : sent + 1].astype(jnp.float32), 0.0)
                total = total + jnp.where(flag > 0, term, 0.0)
            if result is None:
                result = jnp.zeros((height, length), jnp.float32)
            if k:
                total = total + result[rows]
            result = lax.dynamic_update_slice(result, total, (at * piece, 0))
            last = result
    return result


def solution(mesh):
    return jax.shard_map(
        functools.partial(shards, mesh),
        mesh=mesh,
        in_specs=(
            P(("groups", "aux"), "orb", None, None, None),
            P(("groups", "aux"), "orb", None),
            P(("groups", "aux"), "orb"),
            P(("groups", "orb"), "sub"),
        ),
        out_specs=P(("groups", "aux", "sub"), "orb"),
        check_vma=False,
    )
```

```python
import functools

import jax
import jax.numpy as jnp
from jax import lax
from jax.experimental import pallas as pl
from jax.experimental.pallas import tpu as pltpu
from jax.sharding import PartitionSpec as P

GROUP = 4
VMEM_LIMIT = 36 * 1024 * 1024
SMALL_VMEM_LIMIT = 20 * 1024 * 1024
COST = 1024
EXTRA = 16


def transform_kernel(order, columns, bounds, x_ref, *refs, parts, last, together):
    coeff_refs, refs = refs[:parts], refs[parts:]
    if last:
        early_ref, out_ref, x_vmem, coeff_vmem, total, sems, x_sems = refs
    else:
        out_ref, x_vmem, coeff_vmem, total, sems, x_sems = refs
    functions, blocks, slots, side, _ = x_ref.shape
    width = coeff_vmem.shape[1]
    top = coeff_vmem.shape[0] // side - 1

    def x_copy(block, i):
        return pltpu.make_async_copy(
            x_ref.at[:, block, order[block, i]], x_vmem.at[block, i], x_sems.at[block, i]
        )

    @pl.when(pl.program_id(0) == 0)
    def _():
        copies, done = [], 0
        for part, ref in enumerate(coeff_refs):
            rows = ref.shape[0]
            copy = pltpu.make_async_copy(ref, coeff_vmem.at[pl.ds(done, rows)], sems.at[part])
            copy.start()
            copies.append(copy)
            done += rows

        @pl.loop(0, blocks)
        def _(block):
            @pl.loop(bounds[block, 0], bounds[block, 1])
            def _(i):
                x_copy(block, i).start()

        for copy in copies:
            copy.wait()

    @pl.loop(0, together)
    def _(inner):
        block = pl.program_id(0) * together + inner
        start = bounds[block, 0]
        count = bounds[block, 1] - start

        @pl.loop(start, bounds[block, 1])
        def _(i):
            x_copy(block, i).wait()

        def product(first, group, masked):
            slot = [jnp.minimum(start + first + t, slots - 1) for t in range(group)]
            left = jnp.concatenate(
                [jnp.concatenate([x_vmem[block, i, p] for i in slot], axis=1) for p in range(functions)],
                axis=0,
            )
            if masked:
                lane = lax.broadcasted_iota(jnp.int32, left.shape, 1)
                left = jnp.where(lane < (count - first) * side, left, jnp.zeros_like(left))
            right = jnp.concatenate(
                [
                    coeff_vmem[pl.ds(pl.multiple_of(jnp.minimum(columns[block, i], top) * side, side), side), :]
                    for i in slot
                ],
                axis=0,
            )
            return jnp.dot(left, right, preferred_element_type=jnp.float32)

        total[...] = early_ref[inner] if last else jnp.zeros_like(total)
        full = lax.div(count, GROUP)
        rest = count - full * GROUP

        @pl.loop(0, full)
        def _(g):
            total[...] += product(g * GROUP, GROUP, False)

        @pl.when(rest > GROUP // 2)
        def _():
            total[...] += product(full * GROUP, GROUP, True)

        @pl.when((rest > 0) & (rest <= GROUP // 2))
        def _():
            total[...] += product(full * GROUP, GROUP // 2, True)

        if last:
            rows = pl.ds(pl.multiple_of(inner * side, side), side)
            for p in range(functions):
                out_ref[rows, p * width : (p + 1) * width] = total[p * side : (p + 1) * side, :].astype(
                    out_ref.dtype
                )
        else:
            out_ref[inner] = total[...]


def transform(three_index, order, columns, bounds, coeff_parts, early=None):
    functions, blocks, slots, side, _ = three_index.shape
    width = coeff_parts[0].shape[1]
    parts = len(coeff_parts)
    together = next(t for t in (2, 1) if blocks % t == 0)
    sums = pl.BlockSpec((together, functions * side, width), lambda m, *_: (m, 0, 0))
    last = early is not None
    return pl.pallas_call(
        functools.partial(transform_kernel, parts=parts, last=last, together=together),
        grid_spec=pltpu.PrefetchScalarGridSpec(
            num_scalar_prefetch=3,
            grid=(blocks // together,),
            in_specs=[pl.BlockSpec(memory_space=pl.ANY)] * (parts + 1) + [sums] * last,
            out_specs=pl.BlockSpec((together * side, functions * width), lambda m, *_: (m, 0)) if last else sums,
            scratch_shapes=[
                pltpu.VMEM((blocks, slots, functions, side, side), jnp.bfloat16),
                pltpu.VMEM((sum(c.shape[0] for c in coeff_parts), width), jnp.bfloat16),
                pltpu.VMEM((functions * side, width), jnp.float32),
                pltpu.SemaphoreType.DMA((parts,)),
                pltpu.SemaphoreType.DMA((blocks, slots)),
            ],
        ),
        out_shape=jax.ShapeDtypeStruct((blocks * side, functions * width), jnp.bfloat16)
        if last
        else jax.ShapeDtypeStruct((blocks, functions * side, width), jnp.float32),
        compiler_params=pltpu.CompilerParams(vmem_limit_bytes=VMEM_LIMIT),
        cost_estimate=pl.CostEstimate(flops=COST, bytes_accessed=COST, transcendentals=0),
    )(order, columns, bounds, three_index, *coeff_parts, *([early] * last))


def collect_kernel(index, *refs):
    for t, ref in enumerate(refs[:-1]):
        refs[-1][t] = ref[0]


def collect(index, views):
    parts = len(views)
    height, depth = views[0].shape[1:]
    tall = height // 2 if height % 256 == 0 else height
    return pl.pallas_call(
        collect_kernel,
        grid_spec=pltpu.PrefetchScalarGridSpec(
            num_scalar_prefetch=1,
            grid=(height // tall,),
            in_specs=[pl.BlockSpec((1, tall, depth), lambda r, index: (index[0], r, 0))] * parts,
            out_specs=pl.BlockSpec((parts, tall, depth), lambda r, index: (0, r, 0)),
        ),
        out_shape=jax.ShapeDtypeStruct((parts, height, depth), views[0].dtype),
        compiler_params=pltpu.CompilerParams(vmem_limit_bytes=SMALL_VMEM_LIMIT),
        cost_estimate=pl.CostEstimate(flops=COST, bytes_accessed=COST, transcendentals=0),
    )(index[None], *views)


def store_rounded(out_ref, total, first_diagonal, carried):
    rows, tile = total.shape
    rounded = total.astype(out_ref.dtype)
    out_ref[:rows] = rounded
    if out_ref.shape[0] == rows:
        return
    row = lax.broadcasted_iota(jnp.int32, total.shape, 0) + first_diagonal
    col = lax.broadcasted_iota(jnp.int32, total.shape, 1) + pl.program_id(0) * tile
    lost = jnp.where(row == col, total - rounded.astype(jnp.float32), 0.0)
    lost = jnp.sum(lost, axis=0, keepdims=True)
    if carried is not None:
        lost = lost + carried
    extra = lax.broadcasted_iota(jnp.int32, (EXTRA, tile), 0)
    out_ref[rows:] = jnp.where(extra == 0, lost, 0.0).astype(out_ref.dtype)


def forward_kernel(flags, *refs, choices, first):
    out_ref = refs[-1]
    for i in range(choices):
        sums_ref, came_ref = refs[2 * i], refs[2 * i + 1]

        @pl.when(flags[i] > 0)
        def _(sums_ref=sums_ref, came_ref=came_ref):
            rows = sums_ref.shape[0]
            total = sums_ref[...] + came_ref[:rows].astype(jnp.float32)
            carried = came_ref[rows : rows + 1].astype(jnp.float32) if came_ref.shape[0] > rows else None
            store_rounded(out_ref, total, flags[choices] + first, carried)


def forward(flags, sums, came, piece, c):
    choices, length = len(sums), sums[0].shape[1]
    tile = min(length, 512)
    sent = came[0].shape[0]
    in_specs, operands = [], []
    for i in range(choices):
        in_specs.append(pl.BlockSpec((piece, tile), lambda j, flags, i=i: (c, j * flags[i])))
        in_specs.append(pl.BlockSpec((sent, tile), lambda j, flags, i=i: (0, j * flags[i])))
        operands += [sums[i], came[i]]
    return pl.pallas_call(
        functools.partial(forward_kernel, choices=choices, first=c * piece),
        grid_spec=pltpu.PrefetchScalarGridSpec(
            num_scalar_prefetch=1,
            grid=(length // tile,),
            in_specs=in_specs,
            out_specs=pl.BlockSpec((sent, tile), lambda j, flags: (0, j)),
        ),
        out_shape=jax.ShapeDtypeStruct(came[0].shape, came[0].dtype),
        compiler_params=pltpu.CompilerParams(vmem_limit_bytes=SMALL_VMEM_LIMIT),
        cost_estimate=pl.CostEstimate(flops=COST, bytes_accessed=COST, transcendentals=0),
    )(flags, *operands)


def fold_kernel(flags, *refs, extra, first):
    before_ref, sums_ref, came_refs, out_ref = refs[0], refs[1], refs[2:-1], refs[-1]
    rows, tile = out_ref.shape
    out_ref[...] = jnp.zeros_like(out_ref) if first else before_ref[...]

    @pl.when(flags[0] > 0)
    def _():
        out_ref[...] += sums_ref[...]

    for i, ref in enumerate(came_refs):

        @pl.when(flags[i + 1] > 0)
        def _(ref=ref):
            term = ref[:rows].astype(jnp.float32)
            if extra:
                row = lax.broadcasted_iota(jnp.int32, (rows, tile), 0) + flags[len(came_refs) + 1]
                col = lax.broadcasted_iota(jnp.int32, (rows, tile), 1) + pl.program_id(0) * tile
                term = term + jnp.where(row == col, ref[rows : rows + 1].astype(jnp.float32), 0.0)
            out_ref[...] += term


def fold(flags, before, sums, came, rows, at, extra, first):
    height, length = before.shape
    tile = min(length, 512)
    in_place = pl.BlockSpec((rows, tile), lambda j, flags: (at, j))
    return pl.pallas_call(
        functools.partial(fold_kernel, extra=extra, first=first),
        grid_spec=pltpu.PrefetchScalarGridSpec(
            num_scalar_prefetch=1,
            grid=(length // tile,),
            in_specs=[
                pl.BlockSpec((rows, tile), lambda j, flags: (at, 0)) if first else in_place,
                pl.BlockSpec((rows, tile), lambda j, flags: (at, j * flags[0])),
            ]
            + [
                pl.BlockSpec((message.shape[0], tile), lambda j, flags, i=i: (0, j * flags[i + 1]))
                for i, message in enumerate(came)
            ],
            out_specs=in_place,
        ),
        out_shape=jax.ShapeDtypeStruct(before.shape, before.dtype),
        input_output_aliases={} if first else {1: 0},
        compiler_params=pltpu.CompilerParams(vmem_limit_bytes=SMALL_VMEM_LIMIT),
        cost_estimate=pl.CostEstimate(flops=COST, bytes_accessed=COST, transcendentals=0),
    )(flags, before, sums, *came)


def product_kernel(index, *refs, parts, extra):
    out_ref, piece_refs = refs[2 * parts], refs[2 * parts + 1 :]
    total = None
    for rows_ref, cols_ref in zip(refs[:parts], refs[parts : 2 * parts]):
        term = lax.dot_general(
            rows_ref[0], cols_ref[...], (((1,), (1,)), ((), ())), preferred_element_type=jnp.float32
        )
        total = term if total is None else total + term
    out_ref[...] = total
    for c, ref in enumerate(piece_refs):
        rows = ref.shape[0] - extra
        store_rounded(ref, total[c * rows : (c + 1) * rows], index[0] * total.shape[0] + c * rows, None)


def row_product(index, rows, cols, pieces, extra, cost):
    parts = len(rows)
    height, depth = rows[0].shape[1:]
    length = cols[0].shape[0]
    tile = min(length, 512)
    taller = height // max(pieces, 1) + extra
    return pl.pallas_call(
        functools.partial(product_kernel, parts=parts, extra=extra),
        grid_spec=pltpu.PrefetchScalarGridSpec(
            num_scalar_prefetch=1,
            grid=(length // tile,),
            in_specs=[
                pl.BlockSpec((1, height, depth), lambda c, index, t=t: (index[t], 0, 0)) for t in range(parts)
            ]
            + [pl.BlockSpec((tile, depth), lambda c, index: (c, 0))] * parts,
            out_specs=[pl.BlockSpec((height, tile), lambda c, index: (0, c))]
            + [pl.BlockSpec((taller, tile), lambda c, index: (0, c))] * pieces,
        ),
        out_shape=[jax.ShapeDtypeStruct((height, length), jnp.float32)]
        + [jax.ShapeDtypeStruct((taller, length), jnp.bfloat16)] * pieces,
        compiler_params=pltpu.CompilerParams(vmem_limit_bytes=SMALL_VMEM_LIMIT),
        cost_estimate=pl.CostEstimate(flops=cost, bytes_accessed=COST, transcendentals=0),
    )(index, *rows, *cols)


class Line:
    def __init__(self, aux, orb):
        self.aux, self.orb, self.owned = aux, orb, aux // orb

    def targets(self, phase, o):
        first = ((o + phase) % self.orb) * self.owned
        return list(range(first, first + self.owned))

    def chains(self, phase, o, direction):
        head = 0 if direction > 0 else self.aux - 1
        found = sorted((t for t in self.targets(phase, o) if t != head), key=lambda t: -t * direction)
        late = self.owned - len(found) if phase else 0
        return {t: place + late for place, t in enumerate(found)}

    def first_use(self, phase, o, z, target):
        if target == z:
            return 10 * self.aux
        direction = 1 if target > z else -1
        return self.chains(phase, o, direction)[target] + (z if direction > 0 else self.aux - 1 - z)

    def order(self, phase, o, z):
        return sorted(self.targets(phase, o), key=lambda d: (self.first_use(phase, o, z, d), d))

    def hop(self, phase, rank, step):
        pairs, position, final = [], {}, {}
        for o in range(self.orb):
            for direction in (1, -1):
                z = step if direction > 0 else self.aux - 1 - step
                for target, place in self.chains(phase, o, direction).items():
                    if place != rank or (target - z) * direction <= 0:
                        continue
                    pairs.append((z * self.orb + o, (z + direction) * self.orb + o))
                    position[z * self.orb + o] = self.order(phase, o, z).index(target)
                    if z + direction == target:
                        final[target * self.orb + o] = True
        return pairs, position, final

    def merged(self, phase):
        groups = []
        for due in range(self.owned + self.aux - 2):
            open_groups = []
            for rank in range(self.owned):
                step = due - rank
                if not 0 <= step < self.aux - 1 or not self.hop(phase, rank, step)[0]:
                    continue
                pairs = self.hop(phase, rank, step)[0]
                for group in open_groups if step >= 1 and due >= 2 else []:
                    others = [p for r, st in group for p in self.hop(phase, r, st)[0]]
                    if not {p[0] for p in pairs} & {p[0] for p in others} and not {p[1] for p in pairs} & {
                        p[1] for p in others
                    }:
                        group.append((rank, step))
                        break
                else:
                    if step >= 1 and due >= 2:
                        open_groups.append([(rank, step)])
                    else:
                        groups.append([(rank, step)])
            groups += open_groups
        return groups


def lookup(table, place):
    return jnp.asarray(table, jnp.int32)[place]


def after(value, earlier):
    return value if earlier is None else lax.optimization_barrier((value, earlier))[0]


def shards(mesh, three_index, block_cols, live_count, coefficients):
    aux, orb, sub = mesh.shape["aux"], mesh.shape["orb"], mesh.shape["sub"]
    z, o, s = lax.axis_index("aux"), lax.axis_index("orb"), lax.axis_index("sub")
    place = z * orb + o
    line = Line(aux, orb)
    owned = line.owned
    blocks = three_index.shape[1]

    side = three_index.shape[3]
    share = blocks // 3 if aux % 2 == 0 else 0
    parity = lax.rem(z, 2)
    firsts, rests = [], []
    for k in range(1, orb):
        pairs = [((t + k) % orb, t) for t in range(orb)]
        if share:
            first = lax.dynamic_slice_in_dim(coefficients, parity * share * side, share * side)
            firsts.append(lax.ppermute(first, "orb", pairs))
        rests.append(lax.ppermute(coefficients[2 * share * side :], "orb", pairs))

    slots = three_index.shape[2]
    all_blocks = blocks * orb
    columns = lax.rem(block_cols[0] - o * blocks + all_blocks, all_blocks)
    slot = lax.broadcasted_iota(jnp.int32, columns.shape, 1)
    alive = slot < live_count[0][:, None]
    mine = columns < blocks
    rank_key = jnp.where(alive, jnp.where(mine, 0, slots), 2 * slots) + slot
    rank = jnp.sum((rank_key[:, None, :] < rank_key[:, :, None]).astype(jnp.int32), axis=2)
    within = lax.rem(columns, blocks)
    half = lax.div(within, max(share, 1))
    moved = jnp.where(
        within >= 2 * share,
        within - share,
        jnp.where(half == parity, within - half * share, within - half * share + blocks - share),
    )
    placed = jnp.where(mine, columns, columns - within - blocks + moved)
    at_rank = rank[:, None, :] == lax.broadcasted_iota(jnp.int32, (1, slots, 1), 1)
    order = jnp.sum(jnp.where(at_rank, slot[:, None, :], 0), axis=2)
    columns = jnp.sum(jnp.where(at_rank, placed[:, None, :], 0), axis=2)
    live = jnp.sum(alive.astype(jnp.int32), axis=1)
    near = jnp.sum((alive & mine).astype(jnp.int32), axis=1)
    bounds = jnp.stack([jnp.zeros_like(near), near], axis=1)
    early = transform(three_index, order, columns, bounds, [coefficients])
    coeff_parts = []
    for k in range(1, orb):
        if not share:
            coeff_parts.append(rests[k - 1])
            continue
        handed = lax.ppermute(after(firsts[k - 1], early), "aux", [(i, i ^ 1) for i in range(aux)])
        coeff_parts += [firsts[k - 1], rests[k - 1], handed]
    if coeff_parts:
        bounds = jnp.stack([near, live], axis=1)
        own = transform(three_index, order, columns, bounds, coeff_parts, early)
    else:
        functions, width = three_index.shape[0], coefficients.shape[1]
        own = early.reshape(blocks, functions, side, width).transpose(0, 2, 1, 3)
        own = own.reshape(blocks * side, functions * width).astype(jnp.bfloat16)
    length, depth = own.shape
    height = length // (owned * sub)
    halves = 2 if height % 256 == 0 else 1

    def pieces(k):
        return halves if k else 1

    cols = [own]
    for t in range(1, sub):
        cols.append(lax.ppermute(own, "sub", [((u + t) % sub, u) for u in range(sub)]))
    views = [c.reshape(owned * sub, height, depth) for c in cols]

    def rows_to_send(k, q, earlier):
        table = [line.order(k, (b - k) % orb, a)[q] % owned for a in range(aux) for b in range(orb)]
        message = collect(after(lookup(table, place) * sub + s, earlier), views)
        return message, lax.ppermute(message, "orb", [((b + k) % orb, b) for b in range(orb)])

    own_blocks = [
        lookup([line.order(0, b, a)[q] % owned for a in range(aux) for b in range(orb)], place) * sub + s
        for q in range(owned)
    ]

    events, finals = [], []
    for k in range(orb):
        base = (owned * k - 1 if k else 0) * halves
        wide = halves // pieces(k)
        ready = [base + q * halves - 0.4 if k else 0.25 * q - 1 for q in range(owned)]
        for q in range(owned):
            if k:
                events.append((-1.1 if q == 0 and k == 1 else -0.7, 0, "rows", k, q, 0))
            events.append((ready[q], 0, "product", k, q, 0))
        for group in line.merged(k):
            step = group[0][1]
            for c in range(pieces(k)):
                when = max(base + rank * halves + (c + st) * wide for rank, st in group)
                if step == 0 and c == 0:
                    when = ready[group[0][0]] + 0.1
                events.append((when, step, "hop", k, tuple(group), c))
            if any(line.hop(k, *member)[2] for member in group):
                finals.append((k, tuple(group)))
    end = max(e[0] for e in events)
    for k in range(orb):
        for c in range(pieces(k)):
            events.append((end + 1 + k, c, "fold", k, c, 0))
    events.sort(key=lambda e: e[:2])

    came_rows, sums, heads, came, result, last = {}, {}, {}, {}, None, None
    for _, _, kind, k, what, c in events:
        extra = 0 if k else EXTRA
        piece = height // pieces(k)
        if kind == "rows":
            last, came_rows[k, what] = rows_to_send(k, what, last)
        elif kind == "product":
            q = what
            if k == 0:
                index = jnp.broadcast_to(own_blocks[q], (sub,))
                rows = views
            else:
                index = jnp.arange(sub, dtype=jnp.int32)
                rows = [came_rows[k, q]] * sub
            flops = 2 * sub * height * length * depth
            sums[k, q], *heads[k, q] = row_product(after(index, last), rows, cols, pieces(k), extra, flops if k else COST)
            last = sums[k, q]
        elif kind == "hop":
            pairs, choices = [], []
            for rank, step in what:
                more, position, _ = line.hop(k, rank, step)
                pairs += more
                for q in sorted(set(position.values())):
                    choices.append((rank, step, q, [position.get(i) == q for i in range(aux * orb)]))
            if step == 0:
                value = heads[k, choices[0][2]][c]
                for _, _, q, table in choices[1:]:
                    value = jnp.where(lookup(table, place) > 0, heads[k, q][c], value)
                value = after(value, last) if c or len(choices) > 1 else value
            else:
                flags = [lookup(table, place) for _, _, _, table in choices]
                start = sum(flag * own_blocks[q] for flag, (_, _, q, _) in zip(flags, choices)) * height
                value = forward(
                    after(jnp.stack(flags + [start]), last),
                    [sums[k, q] for _, _, q, _ in choices],
                    [came[k, rank, step - 1, c] for rank, step, _, _ in choices],
                    piece,
                    c,
                )
            last = value
            arrived = lax.ppermute(value, ("aux", "orb"), pairs)
            for rank, step in what:
                came[k, rank, step, c] = arrived
        else:
            flags = [[z_ in line.targets(k, o_) for z_ in range(aux) for o_ in range(orb)]]
            parts = []
            for k_, group in finals:
                if k_ == k:
                    places = {i for member in group for i in line.hop(k, *member)[2]}
                    flags.append([i in places for i in range(aux * orb)])
                    parts.append(came[(k,) + group[0] + (what,)])
            flags = [lookup(table, place) for table in flags]
            flags = jnp.stack(flags + [(lax.rem(z, owned) * sub + s) * height + what * piece])
            mine = sums[k, owned - 1]
            before = mine if result is None else result
            result = fold(after(flags, last), before, mine, parts, piece, what, extra, result is None)
            last = result
    return result


def solution(mesh):
    return jax.shard_map(
        functools.partial(shards, mesh),
        mesh=mesh,
        in_specs=(
            P(("groups", "aux"), "orb", None, None, None),
            P(("groups", "aux"), "orb", None),
            P(("groups", "aux"), "orb"),
            P(("groups", "orb"), "sub"),
        ),
        out_specs=P(("groups", "aux", "sub"), "orb"),
        check_vma=False,
    )
```

```python
import functools

import jax
import jax.numpy as jnp
from jax import lax
from jax.experimental import pallas as pl
from jax.experimental.pallas import tpu as pltpu
from jax.sharding import PartitionSpec as P

GROUP = 4
VMEM_LIMIT = 58 * 1024 * 1024
COST = 1024
FORWARD_COST = 4 * 10**9
EXTRA = 16


def transform_kernel(order, columns, bounds, x_ref, *refs, parts, last, together):
    coeff_refs, refs = refs[:parts], refs[parts:]
    if last:
        early_ref, out_ref, x_vmem, coeff_vmem, total, sems, x_sems = refs
    else:
        out_ref, x_vmem, coeff_vmem, total, sems, x_sems = refs
    functions, blocks, slots, side, _ = x_ref.shape
    width = coeff_vmem.shape[1]
    top = coeff_vmem.shape[0] // side - 1

    def x_copy(block, i):
        return pltpu.make_async_copy(
            x_ref.at[:, block, order[block, i]], x_vmem.at[block, i], x_sems.at[block, i]
        )

    @pl.when(pl.program_id(0) == 0)
    def _():
        copies, done = [], 0
        for part, ref in enumerate(coeff_refs):
            rows = ref.shape[0]
            copy = pltpu.make_async_copy(ref, coeff_vmem.at[pl.ds(done, rows)], sems.at[part])
            copy.start()
            copies.append(copy)
            done += rows

        @pl.loop(0, blocks)
        def _(block):
            @pl.loop(bounds[block, 0], bounds[block, 1])
            def _(i):
                x_copy(block, i).start()

        for copy in copies:
            copy.wait()

    @pl.loop(0, together)
    def _(inner):
        block = pl.program_id(0) * together + inner
        start = bounds[block, 0]
        count = bounds[block, 1] - start

        @pl.loop(start, bounds[block, 1])
        def _(i):
            x_copy(block, i).wait()

        def product(first, group, masked):
            slot = [jnp.minimum(start + first + t, slots - 1) for t in range(group)]
            left = jnp.concatenate(
                [jnp.concatenate([x_vmem[block, i, p] for i in slot], axis=1) for p in range(functions)],
                axis=0,
            )
            if masked:
                lane = lax.broadcasted_iota(jnp.int32, left.shape, 1)
                left = jnp.where(lane < (count - first) * side, left, jnp.zeros_like(left))
            right = jnp.concatenate(
                [
                    coeff_vmem[pl.ds(pl.multiple_of(jnp.minimum(columns[block, i], top) * side, side), side), :]
                    for i in slot
                ],
                axis=0,
            )
            return jnp.dot(left, right, preferred_element_type=jnp.float32)

        total[...] = early_ref[inner] if last else jnp.zeros_like(total)
        full = lax.div(count, GROUP)
        rest = count - full * GROUP

        @pl.loop(0, full)
        def _(g):
            total[...] += product(g * GROUP, GROUP, False)

        @pl.when(rest > GROUP // 2)
        def _():
            total[...] += product(full * GROUP, GROUP, True)

        @pl.when((rest > 0) & (rest <= GROUP // 2))
        def _():
            total[...] += product(full * GROUP, GROUP // 2, True)

        if last:
            rows = pl.ds(pl.multiple_of(inner * side, side), side)
            for p in range(functions):
                out_ref[rows, p * width : (p + 1) * width] = total[p * side : (p + 1) * side, :].astype(
                    out_ref.dtype
                )
        else:
            out_ref[inner] = total[...]


def transform(three_index, order, columns, bounds, coeff_parts, early=None):
    functions, blocks, slots, side, _ = three_index.shape
    width = coeff_parts[0].shape[1]
    parts = len(coeff_parts)
    together = next(t for t in (4, 2, 1) if blocks % t == 0)
    sums = pl.BlockSpec((together, functions * side, width), lambda m, *_: (m, 0, 0))
    last = early is not None
    return pl.pallas_call(
        functools.partial(transform_kernel, parts=parts, last=last, together=together),
        grid_spec=pltpu.PrefetchScalarGridSpec(
            num_scalar_prefetch=3,
            grid=(blocks // together,),
            in_specs=[pl.BlockSpec(memory_space=pl.ANY)] * (parts + 1) + [sums] * last,
            out_specs=pl.BlockSpec((together * side, functions * width), lambda m, *_: (m, 0)) if last else sums,
            scratch_shapes=[
                pltpu.VMEM((blocks, slots, functions, side, side), jnp.bfloat16),
                pltpu.VMEM((sum(c.shape[0] for c in coeff_parts), width), jnp.bfloat16),
                pltpu.VMEM((functions * side, width), jnp.float32),
                pltpu.SemaphoreType.DMA((parts,)),
                pltpu.SemaphoreType.DMA((blocks, slots)),
            ],
        ),
        out_shape=jax.ShapeDtypeStruct((blocks * side, functions * width), jnp.bfloat16)
        if last
        else jax.ShapeDtypeStruct((blocks, functions * side, width), jnp.float32),
        compiler_params=pltpu.CompilerParams(vmem_limit_bytes=VMEM_LIMIT),
        cost_estimate=pl.CostEstimate(flops=COST, bytes_accessed=COST, transcendentals=0),
    )(order, columns, bounds, three_index, *coeff_parts, *([early] * last))


def collect_kernel(index, *refs):
    for t, ref in enumerate(refs[:-1]):
        refs[-1][t] = ref[0]


def collect(index, at, views):
    parts = len(views)
    height, depth = views[0].shape[1:]
    tall = height // 2 if height % 256 == 0 else height
    return pl.pallas_call(
        collect_kernel,
        grid_spec=pltpu.PrefetchScalarGridSpec(
            num_scalar_prefetch=1,
            grid=(height // tall,),
            in_specs=[pl.BlockSpec((1, tall, depth), lambda r, index: (index[at], r, 0))] * parts,
            out_specs=pl.BlockSpec((parts, tall, depth), lambda r, index: (0, r, 0)),
        ),
        out_shape=jax.ShapeDtypeStruct((parts, height, depth), views[0].dtype),
        compiler_params=pltpu.CompilerParams(vmem_limit_bytes=VMEM_LIMIT),
        cost_estimate=pl.CostEstimate(flops=COST, bytes_accessed=COST, transcendentals=0),
    )(index, *views)


def store_rounded(out_ref, total, first_diagonal, carried):
    rows, tile = total.shape
    rounded = total.astype(out_ref.dtype)
    out_ref[:rows] = rounded
    if out_ref.shape[0] == rows:
        return
    row = lax.broadcasted_iota(jnp.int32, total.shape, 0) + first_diagonal
    col = lax.broadcasted_iota(jnp.int32, total.shape, 1) + pl.program_id(0) * tile
    lost = jnp.where(row == col, total - rounded.astype(jnp.float32), 0.0)
    lost = jnp.sum(lost, axis=0, keepdims=True)
    if carried is not None:
        lost = lost + carried
    extra = lax.broadcasted_iota(jnp.int32, (EXTRA, tile), 0)
    out_ref[rows:] = jnp.where(extra == 0, lost, 0.0).astype(out_ref.dtype)


def forward_kernel(flags, *refs, at, choices, first):
    out_ref = refs[-1]
    for i in range(choices):
        sums_ref, came_ref = refs[2 * i], refs[2 * i + 1]

        @pl.when(flags[at + i] > 0)
        def _(sums_ref=sums_ref, came_ref=came_ref):
            rows = sums_ref.shape[0]
            total = sums_ref[...] + came_ref[:rows].astype(jnp.float32)
            carried = came_ref[rows : rows + 1].astype(jnp.float32) if came_ref.shape[0] > rows else None
            store_rounded(out_ref, total, flags[at + choices] + first, carried)


def forward(flags, at, sums, came, piece, c, cost):
    choices, length = len(sums), sums[0].shape[1]
    tile = min(length, 1024)
    sent = came[0].shape[0]
    in_specs, operands = [], []
    for i in range(choices):
        in_specs.append(pl.BlockSpec((piece, tile), lambda j, flags, i=i: (c, j * flags[at + i])))
        in_specs.append(pl.BlockSpec((sent, tile), lambda j, flags, i=i: (0, j * flags[at + i])))
        operands += [sums[i], came[i]]
    return pl.pallas_call(
        functools.partial(forward_kernel, at=at, choices=choices, first=c * piece),
        grid_spec=pltpu.PrefetchScalarGridSpec(
            num_scalar_prefetch=1,
            grid=(length // tile,),
            in_specs=in_specs,
            out_specs=pl.BlockSpec((sent, tile), lambda j, flags: (0, j)),
        ),
        out_shape=jax.ShapeDtypeStruct(came[0].shape, came[0].dtype),
        compiler_params=pltpu.CompilerParams(vmem_limit_bytes=VMEM_LIMIT),
        cost_estimate=pl.CostEstimate(flops=cost, bytes_accessed=COST, transcendentals=0),
    )(flags, *operands)


def fold_kernel(flags, *refs, at, extra, first):
    before_ref, sums_ref, came_refs, out_ref = refs[0], refs[1], refs[2:-1], refs[-1]
    rows, tile = out_ref.shape
    total = jnp.where(flags[at] > 0, sums_ref[...], 0.0)
    if not first:
        total = total + before_ref[...]
    lost = jnp.zeros((1, tile), jnp.float32)
    for i, ref in enumerate(came_refs):
        total = total + jnp.where(flags[at + i + 1] > 0, ref[:rows].astype(jnp.float32), 0.0)
        if extra:
            lost = lost + jnp.where(flags[at + i + 1] > 0, ref[rows : rows + 1].astype(jnp.float32), 0.0)
    if extra:
        row = lax.broadcasted_iota(jnp.int32, (rows, tile), 0) + flags[at + len(came_refs) + 1]
        col = lax.broadcasted_iota(jnp.int32, (rows, tile), 1) + pl.program_id(0) * tile
        total = total + jnp.where(row == col, lost, 0.0)
    out_ref[...] = total


def fold(flags, at, before, sums, came, rows, piece, extra, first):
    height, length = before.shape
    tile = min(length, 1024)
    in_place = pl.BlockSpec((rows, tile), lambda j, flags: (piece, j))
    return pl.pallas_call(
        functools.partial(fold_kernel, at=at, extra=extra, first=first),
        grid_spec=pltpu.PrefetchScalarGridSpec(
            num_scalar_prefetch=1,
            grid=(length // tile,),
            in_specs=[
                pl.BlockSpec((rows, tile), lambda j, flags: (piece, 0)) if first else in_place,
                pl.BlockSpec((rows, tile), lambda j, flags: (piece, j * flags[at])),
            ]
            + [
                pl.BlockSpec((message.shape[0], tile), lambda j, flags, i=i: (0, j * flags[at + i + 1]))
                for i, message in enumerate(came)
            ],
            out_specs=in_place,
        ),
        out_shape=jax.ShapeDtypeStruct(before.shape, before.dtype),
        input_output_aliases={} if first else {1: 0},
        compiler_params=pltpu.CompilerParams(vmem_limit_bytes=VMEM_LIMIT),
        cost_estimate=pl.CostEstimate(flops=COST, bytes_accessed=COST, transcendentals=0),
    )(flags, before, sums, *came)


def product_kernel(index, *refs, at, parts, extra):
    out_ref, piece_refs = refs[2 * parts], refs[2 * parts + 1 :]
    total = None
    for rows_ref, cols_ref in zip(refs[:parts], refs[parts : 2 * parts]):
        term = lax.dot_general(
            rows_ref[0], cols_ref[...], (((1,), (1,)), ((), ())), preferred_element_type=jnp.float32
        )
        total = term if total is None else total + term
    out_ref[...] = total
    for c, ref in enumerate(piece_refs):
        rows = ref.shape[0] - extra
        store_rounded(ref, total[c * rows : (c + 1) * rows], index[at] * total.shape[0] + c * rows, None)


def row_product(index, at, rows, cols, pieces, extra, cost):
    parts = len(rows)
    height, depth = rows[0].shape[1:]
    length = cols[0].shape[0]
    tile = min(length, 512)
    taller = height // max(pieces, 1) + extra
    return pl.pallas_call(
        functools.partial(product_kernel, at=at, parts=parts, extra=extra),
        grid_spec=pltpu.PrefetchScalarGridSpec(
            num_scalar_prefetch=1,
            grid=(length // tile,),
            in_specs=[
                pl.BlockSpec((1, height, depth), lambda c, index, t=t: (index[at + t], 0, 0)) for t in range(parts)
            ]
            + [pl.BlockSpec((tile, depth), lambda c, index: (c, 0))] * parts,
            out_specs=[pl.BlockSpec((height, tile), lambda c, index: (0, c))]
            + [pl.BlockSpec((taller, tile), lambda c, index: (0, c))] * pieces,
        ),
        out_shape=[jax.ShapeDtypeStruct((height, length), jnp.float32)]
        + [jax.ShapeDtypeStruct((taller, length), jnp.bfloat16)] * pieces,
        compiler_params=pltpu.CompilerParams(vmem_limit_bytes=VMEM_LIMIT),
        cost_estimate=pl.CostEstimate(flops=cost, bytes_accessed=COST, transcendentals=0),
    )(index, *rows, *cols)


class Line:
    def __init__(self, aux, orb):
        self.aux, self.orb, self.owned = aux, orb, aux // orb

    def targets(self, phase, o):
        first = ((o + phase) % self.orb) * self.owned
        return list(range(first, first + self.owned))

    def chains(self, phase, o, direction):
        head = 0 if direction > 0 else self.aux - 1
        found = sorted((t for t in self.targets(phase, o) if t != head), key=lambda t: -t * direction)
        late = self.owned - len(found) if phase else 0
        return {t: place + late for place, t in enumerate(found)}

    def first_use(self, phase, o, z, target):
        if target == z:
            return 10 * self.aux
        direction = 1 if target > z else -1
        return self.chains(phase, o, direction)[target] + (z if direction > 0 else self.aux - 1 - z)

    def order(self, phase, o, z):
        return sorted(self.targets(phase, o), key=lambda d: (self.first_use(phase, o, z, d), d))

    def hop(self, phase, rank, step):
        pairs, position, final = [], {}, {}
        for o in range(self.orb):
            for direction in (1, -1):
                z = step if direction > 0 else self.aux - 1 - step
                for target, place in self.chains(phase, o, direction).items():
                    if place != rank or (target - z) * direction <= 0:
                        continue
                    pairs.append((z * self.orb + o, (z + direction) * self.orb + o))
                    position[z * self.orb + o] = self.order(phase, o, z).index(target)
                    if z + direction == target:
                        final[target * self.orb + o] = True
        return pairs, position, final

    def merged(self, phase):
        groups = []
        for due in range(self.owned + self.aux - 2):
            open_groups = []
            for rank in range(self.owned):
                step = due - rank
                if not 0 <= step < self.aux - 1 or not self.hop(phase, rank, step)[0]:
                    continue
                pairs = self.hop(phase, rank, step)[0]
                for group in open_groups if step >= 1 and due >= 2 and phase == 0 else []:
                    others = [p for r, st in group for p in self.hop(phase, r, st)[0]]
                    if not {p[0] for p in pairs} & {p[0] for p in others} and not {p[1] for p in pairs} & {
                        p[1] for p in others
                    }:
                        group.append((rank, step))
                        break
                else:
                    if step >= 1 and due >= 2:
                        open_groups.append([(rank, step)])
                    else:
                        groups.append([(rank, step)])
            groups += open_groups
        return groups


def lookup(table, place):
    return jnp.asarray(table, jnp.int32)[place]


def after(value, earlier):
    return value if earlier is None else lax.optimization_barrier((value, earlier))[0]


def shards(mesh, three_index, block_cols, live_count, coefficients):
    aux, orb, sub = mesh.shape["aux"], mesh.shape["orb"], mesh.shape["sub"]
    z, o, s = lax.axis_index("aux"), lax.axis_index("orb"), lax.axis_index("sub")
    place = z * orb + o
    line = Line(aux, orb)
    owned = line.owned
    blocks = three_index.shape[1]

    side = three_index.shape[3]
    share = blocks // 3 if aux % 2 == 0 else 0
    parity = lax.rem(z, 2)
    firsts, rests = [], []
    for k in range(1, orb):
        pairs = [((t + k) % orb, t) for t in range(orb)]
        if share:
            first = lax.dynamic_slice_in_dim(coefficients, parity * share * side, share * side)
            firsts.append(lax.ppermute(first, "orb", pairs))
        rests.append(lax.ppermute(coefficients[2 * share * side :], "orb", pairs))

    slots = three_index.shape[2]
    all_blocks = blocks * orb
    columns = lax.rem(block_cols[0] - o * blocks + all_blocks, all_blocks)
    slot = lax.broadcasted_iota(jnp.int32, columns.shape, 1)
    alive = slot < live_count[0][:, None]
    mine = columns < blocks
    rank_key = jnp.where(alive, jnp.where(mine, 0, slots), 2 * slots) + slot
    rank = jnp.sum((rank_key[:, None, :] < rank_key[:, :, None]).astype(jnp.int32), axis=2)
    within = lax.rem(columns, blocks)
    half = lax.div(within, max(share, 1))
    moved = jnp.where(
        within >= 2 * share,
        within - share,
        jnp.where(half == parity, within - half * share, within - half * share + blocks - share),
    )
    placed = jnp.where(mine, columns, columns - within - blocks + moved)
    at_rank = rank[:, None, :] == lax.broadcasted_iota(jnp.int32, (1, slots, 1), 1)
    order = jnp.sum(jnp.where(at_rank, slot[:, None, :], 0), axis=2)
    columns = jnp.sum(jnp.where(at_rank, placed[:, None, :], 0), axis=2)
    live = jnp.sum(alive.astype(jnp.int32), axis=1)
    near = jnp.sum((alive & mine).astype(jnp.int32), axis=1)
    bounds = jnp.stack([jnp.zeros_like(near), near], axis=1)
    early = transform(three_index, order, columns, bounds, [coefficients])
    coeff_parts = []
    for k in range(1, orb):
        if not share:
            coeff_parts.append(rests[k - 1])
            continue
        handed = lax.ppermute(after(firsts[k - 1], early), "aux", [(i, i ^ 1) for i in range(aux)])
        coeff_parts += [firsts[k - 1], rests[k - 1], handed]
    if coeff_parts:
        bounds = jnp.stack([near, live], axis=1)
        own = transform(three_index, order, columns, bounds, coeff_parts, early)
    else:
        functions, width = three_index.shape[0], coefficients.shape[1]
        own = early.reshape(blocks, functions, side, width).transpose(0, 2, 1, 3)
        own = own.reshape(blocks * side, functions * width).astype(jnp.bfloat16)
    length, depth = own.shape
    height = length // (owned * sub)
    halves = 2 if height % 256 == 0 else 1

    def pieces(k):
        return halves if k else 1

    cols = [own]
    for t in range(1, sub):
        cols.append(lax.ppermute(own, "sub", [((u + t) % sub, u) for u in range(sub)]))
    views = [c.reshape(owned * sub, height, depth) for c in cols]

    places = [(a, b, c) for a in range(aux) for b in range(orb) for c in range(sub)]
    table = [[] for _ in places]

    def scalars(rows):
        at = len(table[0])
        for line_, row in zip(table, rows):
            line_.extend(int(value) for value in row)
        return at

    def own_block(a, b, c, q):
        return line.order(0, b, a)[q] % owned * sub + c

    events, finals = [], []
    for k in range(orb):
        base = (owned * k - 1 if k else 0) * halves
        wide = halves // pieces(k)
        ready = [base + q * halves - 0.4 if k else 0.25 * q - 1 for q in range(owned)]
        for q in range(owned):
            if k:
                events.append((-1.1 if q == 0 and k == 1 else -0.7, 0, "rows", k, q, 0))
            events.append((ready[q], 0, "product", k, q, 0))
        for group in line.merged(k):
            step = group[0][1]
            for c in range(pieces(k)):
                when = max(base + rank * halves + (c + st) * wide for rank, st in group)
                if step == 0 and c == 0:
                    when = ready[group[0][0]] + 0.1
                if not k and len(group) > 1:
                    when += 0.5
                events.append((when, step, "hop", k, tuple(group), c))
            if any(line.hop(k, *member)[2] for member in group):
                finals.append((k, tuple(group)))
    end = max(e[0] for e in events)
    for k in range(orb):
        for c in range(pieces(k)):
            events.append((end + 1 + k, c, "fold", k, c, 0))
    events.sort(key=lambda e: e[:2])

    plans = []
    for _, _, kind, k, what, c in events:
        piece = height // pieces(k)
        plan = dict(kind=kind, k=k, what=what, c=c)
        if kind == "rows":
            rows = [[line.order(k, (b - k) % orb, a)[what] % owned * sub + d] for a, b, d in places]
        elif kind == "product":
            rows = [[t if k else own_block(a, b, d, what) for t in range(sub)] for a, b, d in places]
        elif kind == "hop":
            pairs, choices, tables = [], [], []
            for rank, step in what:
                more, position, _ = line.hop(k, rank, step)
                pairs += more
                for q in sorted(set(position.values())):
                    choices.append((rank, step, q))
                    tables.append([position.get(a * orb + b) == q for a, b, _ in places])
            plan.update(pairs=pairs, choices=choices)
            rows = []
            for i, (a, b, d) in enumerate(places):
                chosen = [t[i] for t in tables]
                start = sum(own_block(a, b, d, q) for (_, _, q), flag in zip(choices, chosen) if flag)
                rows.append(chosen + [start * height])
        else:
            groups = [group for k_, group in finals if k_ == k]
            ends = [{i for member in group for i in line.hop(k, *member)[2]} for group in groups]
            plan.update(groups=groups)
            rows = [
                [a in line.targets(k, b)]
                + [a * orb + b in end_ for end_ in ends]
                + [(a % owned * sub + d) * height + what * piece]
                for a, b, d in places
            ]
        plan.update(at=scalars(rows), piece=piece)
        plans.append(plan)
    everywhere = lookup(table, place * sub + s)

    came_rows, sums, heads, came, result, last = {}, {}, {}, {}, None, None
    for plan in plans:
        k, what, c, at, piece = (plan[name] for name in ("k", "what", "c", "at", "piece"))
        extra = 0 if k else EXTRA
        if plan["kind"] == "rows":
            last = collect(after(everywhere, last), at, views)
            pairs = [((b + k) % orb, b) for b in range(orb)]
            came_rows[k, what] = lax.ppermute(last, "orb", pairs)
        elif plan["kind"] == "product":
            rows = [came_rows[k, what]] * sub if k else views
            flops = 2 * sub * height * length * depth if k and what == 0 else COST
            sums[k, what], *heads[k, what] = row_product(
                after(everywhere, last), at, rows, cols, pieces(k), extra, flops
            )
            last = sums[k, what]
        elif plan["kind"] == "hop":
            choices = plan["choices"]
            if choices[0][1] == 0:
                value = heads[k, choices[0][2]][c]
                for i, (_, _, q) in enumerate(choices[1:]):
                    value = jnp.where(everywhere[at + 1 + i] > 0, heads[k, q][c], value)
                value = after(value, last) if c or len(choices) > 1 else value
            else:
                value = forward(
                    after(everywhere, last),
                    at,
                    [sums[k, q] for _, _, q in choices],
                    [came[k, rank, step - 1, c] for rank, step, _ in choices],
                    piece,
                    c,
                    FORWARD_COST if k and c == 0 and choices[0][:2] == (0, 1) else COST,
                )
            last = value
            arrived = lax.ppermute(value, ("aux", "orb"), plan["pairs"])
            for member in what:
                came[(k,) + member + (c,)] = arrived
        else:
            messages = [came[(k,) + group[0] + (what,)] for group in plan["groups"]]
            mine = sums[k, owned - 1]
            before = mine if result is None else result
            result = fold(after(everywhere, last), at, before, mine, messages, piece, what, extra, result is None)
            last = result
    return result


def solution(mesh):
    return jax.shard_map(
        functools.partial(shards, mesh),
        mesh=mesh,
        in_specs=(
            P(("groups", "aux"), "orb", None, None, None),
            P(("groups", "aux"), "orb", None),
            P(("groups", "aux"), "orb"),
            P(("groups", "orb"), "sub"),
        ),
        out_specs=P(("groups", "aux", "sub"), "orb"),
        check_vma=False,
    )
```

```python
import functools

import jax
import jax.numpy as jnp
from jax import lax
from jax.experimental import pallas as pl
from jax.experimental.pallas import tpu as pltpu
from jax.sharding import PartitionSpec as P

GROUP = 4
VMEM_LIMIT = 58 * 1024 * 1024
COST = 1024
FORWARD_COST = 4 * 10**9
EXTRA = 16


def transform_kernel(order, columns, bounds, x_ref, *refs, parts, last, together):
    coeff_refs, refs = refs[:parts], refs[parts:]
    if last:
        early_ref, out_ref, x_vmem, coeff_vmem, total, sems, x_sems = refs
    else:
        out_ref, x_vmem, coeff_vmem, total, sems, x_sems = refs
    functions, blocks, slots, side, _ = x_ref.shape
    width = coeff_vmem.shape[1]
    top = coeff_vmem.shape[0] // side - 1

    def x_copy(block, i):
        return pltpu.make_async_copy(
            x_ref.at[:, block, order[block, i]], x_vmem.at[block, i], x_sems.at[block, i]
        )

    @pl.when(pl.program_id(0) == 0)
    def _():
        copies, done = [], 0
        for part, ref in enumerate(coeff_refs):
            rows = ref.shape[0]
            copy = pltpu.make_async_copy(ref, coeff_vmem.at[pl.ds(done, rows)], sems.at[part])
            copy.start()
            copies.append(copy)
            done += rows

        @pl.loop(0, blocks)
        def _(block):
            @pl.loop(bounds[block, 0], bounds[block, 1])
            def _(i):
                x_copy(block, i).start()

        for copy in copies:
            copy.wait()

    @pl.loop(0, together)
    def _(inner):
        block = pl.program_id(0) * together + inner
        start = bounds[block, 0]
        count = bounds[block, 1] - start

        @pl.loop(start, bounds[block, 1])
        def _(i):
            x_copy(block, i).wait()

        def product(first, group, masked):
            slot = [jnp.minimum(start + first + t, slots - 1) for t in range(group)]
            left = jnp.concatenate(
                [jnp.concatenate([x_vmem[block, i, p] for i in slot], axis=1) for p in range(functions)],
                axis=0,
            )
            if masked:
                lane = lax.broadcasted_iota(jnp.int32, left.shape, 1)
                left = jnp.where(lane < (count - first) * side, left, jnp.zeros_like(left))
            right = jnp.concatenate(
                [
                    coeff_vmem[pl.ds(pl.multiple_of(jnp.minimum(columns[block, i], top) * side, side), side), :]
                    for i in slot
                ],
                axis=0,
            )
            return jnp.dot(left, right, preferred_element_type=jnp.float32)

        def emit(value):
            if not last:
                out_ref[inner] = value
                return
            rows = pl.ds(pl.multiple_of(inner * side, side), side)
            for p in range(functions):
                out_ref[rows, p * width : (p + 1) * width] = value[p * side : (p + 1) * side, :].astype(
                    out_ref.dtype
                )

        def begin(value):
            return early_ref[inner] + value if last else value

        @pl.when(count == 0)
        def _():
            emit(begin(jnp.zeros_like(total)))

        @pl.when((count > 0) & (count <= GROUP // 2))
        def _():
            emit(begin(product(0, GROUP // 2, True)))

        @pl.when((count > GROUP // 2) & (count <= GROUP))
        def _():
            emit(begin(product(0, GROUP, True)))

        @pl.when(count > GROUP)
        def _():
            total[...] = begin(product(0, GROUP, False))
            groups = lax.div(count - 1, GROUP)

            @pl.loop(1, groups)
            def _(g):
                total[...] += product(g * GROUP, GROUP, False)

            emit(total[...] + product(groups * GROUP, GROUP, True))


def transform(three_index, order, columns, bounds, coeff_parts, early=None):
    functions, blocks, slots, side, _ = three_index.shape
    width = coeff_parts[0].shape[1]
    parts = len(coeff_parts)
    together = next(t for t in (4, 2, 1) if blocks % t == 0)
    sums = pl.BlockSpec((together, functions * side, width), lambda m, *_: (m, 0, 0))
    last = early is not None
    return pl.pallas_call(
        functools.partial(transform_kernel, parts=parts, last=last, together=together),
        grid_spec=pltpu.PrefetchScalarGridSpec(
            num_scalar_prefetch=3,
            grid=(blocks // together,),
            in_specs=[pl.BlockSpec(memory_space=pl.ANY)] * (parts + 1) + [sums] * last,
            out_specs=pl.BlockSpec((together * side, functions * width), lambda m, *_: (m, 0)) if last else sums,
            scratch_shapes=[
                pltpu.VMEM((blocks, slots, functions, side, side), jnp.bfloat16),
                pltpu.VMEM((sum(c.shape[0] for c in coeff_parts), width), jnp.bfloat16),
                pltpu.VMEM((functions * side, width), jnp.float32),
                pltpu.SemaphoreType.DMA((parts,)),
                pltpu.SemaphoreType.DMA((blocks, slots)),
            ],
        ),
        out_shape=jax.ShapeDtypeStruct((blocks * side, functions * width), jnp.bfloat16)
        if last
        else jax.ShapeDtypeStruct((blocks, functions * side, width), jnp.float32),
        compiler_params=pltpu.CompilerParams(vmem_limit_bytes=VMEM_LIMIT),
        cost_estimate=pl.CostEstimate(flops=COST, bytes_accessed=COST, transcendentals=0),
    )(order, columns, bounds, three_index, *coeff_parts, *([early] * last))


def collect_kernel(index, *refs):
    for t, ref in enumerate(refs[:-1]):
        refs[-1][t] = ref[0]


def collect(index, at, views):
    parts = len(views)
    height, depth = views[0].shape[1:]
    tall = height // 2 if height % 256 == 0 else height
    return pl.pallas_call(
        collect_kernel,
        grid_spec=pltpu.PrefetchScalarGridSpec(
            num_scalar_prefetch=1,
            grid=(height // tall,),
            in_specs=[pl.BlockSpec((1, tall, depth), lambda r, index: (index[at], r, 0))] * parts,
            out_specs=pl.BlockSpec((parts, tall, depth), lambda r, index: (0, r, 0)),
        ),
        out_shape=jax.ShapeDtypeStruct((parts, height, depth), views[0].dtype),
        compiler_params=pltpu.CompilerParams(vmem_limit_bytes=VMEM_LIMIT),
        cost_estimate=pl.CostEstimate(flops=COST, bytes_accessed=COST, transcendentals=0),
    )(index, *views)


def store_rounded(out_ref, total, first_diagonal, carried):
    rows, tile = total.shape
    rounded = total.astype(out_ref.dtype)
    out_ref[:rows] = rounded
    if out_ref.shape[0] == rows:
        return
    row = lax.broadcasted_iota(jnp.int32, total.shape, 0) + first_diagonal
    col = lax.broadcasted_iota(jnp.int32, total.shape, 1) + pl.program_id(0) * tile
    lost = jnp.where(row == col, total - rounded.astype(jnp.float32), 0.0)
    lost = jnp.sum(lost, axis=0, keepdims=True)
    if carried is not None:
        lost = lost + carried
    extra = lax.broadcasted_iota(jnp.int32, (EXTRA, tile), 0)
    out_ref[rows:] = jnp.where(extra == 0, lost, 0.0).astype(out_ref.dtype)


def forward_kernel(flags, *refs, at, choices, first):
    out_ref = refs[-1]
    for i in range(choices):
        sums_ref, came_ref = refs[2 * i], refs[2 * i + 1]

        @pl.when(flags[at + i] > 0)
        def _(sums_ref=sums_ref, came_ref=came_ref):
            rows = sums_ref.shape[0]
            total = sums_ref[...] + came_ref[:rows].astype(jnp.float32)
            carried = came_ref[rows : rows + 1].astype(jnp.float32) if came_ref.shape[0] > rows else None
            store_rounded(out_ref, total, flags[at + choices] + first, carried)


def forward(flags, at, sums, came, piece, c, cost):
    choices, length = len(sums), sums[0].shape[1]
    tile = min(length, 1024)
    sent = came[0].shape[0]
    in_specs, operands = [], []
    for i in range(choices):
        in_specs.append(pl.BlockSpec((piece, tile), lambda j, flags, i=i: (c, j * flags[at + i])))
        in_specs.append(pl.BlockSpec((sent, tile), lambda j, flags, i=i: (0, j * flags[at + i])))
        operands += [sums[i], came[i]]
    return pl.pallas_call(
        functools.partial(forward_kernel, at=at, choices=choices, first=c * piece),
        grid_spec=pltpu.PrefetchScalarGridSpec(
            num_scalar_prefetch=1,
            grid=(length // tile,),
            in_specs=in_specs,
            out_specs=pl.BlockSpec((sent, tile), lambda j, flags: (0, j)),
        ),
        out_shape=jax.ShapeDtypeStruct(came[0].shape, came[0].dtype),
        compiler_params=pltpu.CompilerParams(vmem_limit_bytes=VMEM_LIMIT),
        cost_estimate=pl.CostEstimate(flops=cost, bytes_accessed=COST, transcendentals=0),
    )(flags, *operands)


def fold_kernel(flags, *refs, at, terms):
    term_refs, out_ref = refs[: len(terms)], refs[-1]
    rows, tile = out_ref.shape
    total = jnp.zeros((rows, tile), jnp.float32)
    lost = jnp.zeros((1, tile), jnp.float32)
    for ref, (flag, is_extra) in zip(term_refs, terms):
        if is_extra:
            lost = lost + jnp.where(flags[at + flag] > 0, ref[:1].astype(jnp.float32), 0.0)
        else:
            total = total + jnp.where(flags[at + flag] > 0, ref[...].astype(jnp.float32), 0.0)
    row = lax.broadcasted_iota(jnp.int32, (rows, tile), 0) + flags[at + max(flag for flag, _ in terms) + 1]
    col = lax.broadcasted_iota(jnp.int32, (rows, tile), 1) + pl.program_id(0) * tile
    out_ref[...] = total + jnp.where(row == col, lost, 0.0)


def fold(flags, at, phases, before, piece, c):
    height, length = phases[0][0].shape
    tile = min(length, 1024)
    operands, in_specs, terms = [], [], []

    def add(array, rows, block, flag, is_extra):
        operands.append(array)
        in_specs.append(pl.BlockSpec((rows, tile), lambda j, flags: (block, j * flags[at + flag])))
        terms.append((flag, is_extra))

    flag = 0
    for sums, messages in phases:
        add(sums, piece, c, flag, False)
        flag += 1
        for message in messages:
            whole = message.shape[0] > piece
            add(message, piece, c if whole else 0, flag, False)
            if message.shape[0] % piece:
                add(message, EXTRA, message.shape[0] // EXTRA - 1, flag, True)
            flag += 1
    again = [] if before is None else [before]
    return pl.pallas_call(
        functools.partial(fold_kernel, at=at, terms=terms),
        grid_spec=pltpu.PrefetchScalarGridSpec(
            num_scalar_prefetch=1,
            grid=(length // tile,),
            in_specs=in_specs + [pl.BlockSpec(memory_space=pl.ANY)] * len(again),
            out_specs=pl.BlockSpec((piece, tile), lambda j, flags: (c, j)),
        ),
        out_shape=jax.ShapeDtypeStruct((height, length), jnp.float32),
        input_output_aliases={1 + len(operands): 0} if again else {},
        compiler_params=pltpu.CompilerParams(vmem_limit_bytes=VMEM_LIMIT),
        cost_estimate=pl.CostEstimate(flops=COST, bytes_accessed=COST, transcendentals=0),
    )(flags, *operands, *again)


def product_kernel(index, *refs, at, parts, extra, begun):
    out_ref, piece_refs = refs[2 * parts + begun], refs[2 * parts + begun + 1 :]
    total = refs[2 * parts][...] if begun else None
    for rows_ref, cols_ref in zip(refs[:parts], refs[parts : 2 * parts]):
        term = lax.dot_general(
            rows_ref[0], cols_ref[...], (((1,), (1,)), ((), ())), preferred_element_type=jnp.float32
        )
        total = term if total is None else total + term
    out_ref[...] = total
    for c, ref in enumerate(piece_refs):
        rows = ref.shape[0] - extra
        store_rounded(ref, total[c * rows : (c + 1) * rows], index[at] * total.shape[0] + c * rows, None)


def row_product(index, at, rows, cols, pieces, extra, cost, early=()):
    parts = len(rows)
    height, depth = rows[0].shape[1:]
    length = cols[0].shape[0]
    tile = min(length, 512)
    taller = height // max(pieces, 1) + extra
    return pl.pallas_call(
        functools.partial(product_kernel, at=at, parts=parts, extra=extra, begun=len(early)),
        grid_spec=pltpu.PrefetchScalarGridSpec(
            num_scalar_prefetch=1,
            grid=(length // tile,),
            in_specs=[
                pl.BlockSpec((1, height, depth), lambda c, index, t=t: (index[at + t], 0, 0)) for t in range(parts)
            ]
            + [pl.BlockSpec((tile, depth), lambda c, index: (c, 0))] * parts
            + [pl.BlockSpec((height, tile), lambda c, index: (0, c))] * len(early),
            out_specs=[pl.BlockSpec((height, tile), lambda c, index: (0, c))]
            + [pl.BlockSpec((taller, tile), lambda c, index: (0, c))] * pieces,
        ),
        out_shape=[jax.ShapeDtypeStruct((height, length), jnp.float32)]
        + [jax.ShapeDtypeStruct((taller, length), jnp.bfloat16)] * pieces,
        compiler_params=pltpu.CompilerParams(vmem_limit_bytes=VMEM_LIMIT),
        cost_estimate=pl.CostEstimate(flops=cost, bytes_accessed=COST, transcendentals=0),
    )(index, *rows, *cols, *early)


class Line:
    def __init__(self, aux, orb):
        self.aux, self.orb, self.owned = aux, orb, aux // orb

    def targets(self, phase, o):
        first = ((o + phase) % self.orb) * self.owned
        return list(range(first, first + self.owned))

    def chains(self, phase, o, direction):
        head = 0 if direction > 0 else self.aux - 1
        found = sorted((t for t in self.targets(phase, o) if t != head), key=lambda t: -t * direction)
        late = self.owned - len(found) if phase else 0
        return {t: place + late for place, t in enumerate(found)}

    def first_use(self, phase, o, z, target):
        if target == z:
            return 10 * self.aux
        direction = 1 if target > z else -1
        return self.chains(phase, o, direction)[target] + (z if direction > 0 else self.aux - 1 - z)

    def order(self, phase, o, z):
        return sorted(self.targets(phase, o), key=lambda d: (self.first_use(phase, o, z, d), d))

    def hop(self, phase, rank, step):
        pairs, position, final = [], {}, {}
        for o in range(self.orb):
            for direction in (1, -1):
                z = step if direction > 0 else self.aux - 1 - step
                for target, place in self.chains(phase, o, direction).items():
                    if place != rank or (target - z) * direction <= 0:
                        continue
                    pairs.append((z * self.orb + o, (z + direction) * self.orb + o))
                    position[z * self.orb + o] = self.order(phase, o, z).index(target)
                    if z + direction == target:
                        final[target * self.orb + o] = True
        return pairs, position, final

    def merged(self, phase):
        groups = []
        for due in range(self.owned + self.aux - 2):
            open_groups = []
            for rank in range(self.owned):
                step = due - rank
                if not 0 <= step < self.aux - 1 or not self.hop(phase, rank, step)[0]:
                    continue
                pairs = self.hop(phase, rank, step)[0]
                for group in open_groups if step >= 1 and due >= 2 and phase == 0 else []:
                    others = [p for r, st in group for p in self.hop(phase, r, st)[0]]
                    if not {p[0] for p in pairs} & {p[0] for p in others} and not {p[1] for p in pairs} & {
                        p[1] for p in others
                    }:
                        group.append((rank, step))
                        break
                else:
                    if step >= 1 and due >= 2:
                        open_groups.append([(rank, step)])
                    else:
                        groups.append([(rank, step)])
            groups += open_groups
        return groups


def lookup(table, place):
    return jnp.asarray(table, jnp.int32)[place]


def after(value, earlier):
    return value if earlier is None else lax.optimization_barrier((value, earlier))[0]


def shards(mesh, three_index, block_cols, live_count, coefficients):
    aux, orb, sub = mesh.shape["aux"], mesh.shape["orb"], mesh.shape["sub"]
    z, o, s = lax.axis_index("aux"), lax.axis_index("orb"), lax.axis_index("sub")
    place = z * orb + o
    line = Line(aux, orb)
    owned = line.owned
    blocks = three_index.shape[1]

    side = three_index.shape[3]
    share = blocks // 3 if aux % 2 == 0 else 0
    parity = lax.rem(z, 2)
    firsts, rests = [], []
    for k in range(1, orb):
        pairs = [((t + k) % orb, t) for t in range(orb)]
        if share:
            first = lax.dynamic_slice_in_dim(coefficients, parity * share * side, share * side)
            firsts.append(lax.ppermute(first, "orb", pairs))
        rests.append(lax.ppermute(coefficients[2 * share * side :], "orb", pairs))

    slots = three_index.shape[2]
    all_blocks = blocks * orb
    columns = lax.rem(block_cols[0] - o * blocks + all_blocks, all_blocks)
    slot = lax.broadcasted_iota(jnp.int32, columns.shape, 1)
    alive = slot < live_count[0][:, None]
    within = lax.rem(columns, blocks)
    shard = lax.div(columns, blocks)
    half = lax.div(within, max(share, 1))
    shared = within < 2 * share
    mine = (shard == 0) | (shared & (half == parity))
    placed = jnp.where(
        shard == 0,
        within,
        jnp.where(
            mine,
            blocks + (shard - 1) * share + within - half * share,
            (shard - 1) * (blocks - share)
            + jnp.where(shared, blocks - 2 * share + within - half * share, within - 2 * share),
        ),
    )
    rank_key = jnp.where(alive, jnp.where(mine, 0, slots), 2 * slots) + slot
    rank = jnp.sum((rank_key[:, None, :] < rank_key[:, :, None]).astype(jnp.int32), axis=2)
    at_rank = rank[:, None, :] == lax.broadcasted_iota(jnp.int32, (1, slots, 1), 1)
    order = jnp.sum(jnp.where(at_rank, slot[:, None, :], 0), axis=2)
    columns = jnp.sum(jnp.where(at_rank, placed[:, None, :], 0), axis=2)
    live = jnp.sum(alive.astype(jnp.int32), axis=1)
    near = jnp.sum((alive & mine).astype(jnp.int32), axis=1)
    bounds = jnp.stack([jnp.zeros_like(near), near], axis=1)
    coeff_parts = []
    for k in range(1, orb):
        coeff_parts.append(rests[k - 1])
        if share:
            coeff_parts.append(lax.ppermute(firsts[k - 1], "aux", [(i, i ^ 1) for i in range(aux)]))
    early = transform(three_index, order, columns, bounds, [coefficients] + firsts)
    if coeff_parts:
        bounds = jnp.stack([near, live], axis=1)
        own = transform(three_index, order, columns, bounds, coeff_parts, early)
    else:
        functions, width = three_index.shape[0], coefficients.shape[1]
        own = early.reshape(blocks, functions, side, width).transpose(0, 2, 1, 3)
        own = own.reshape(blocks * side, functions * width).astype(jnp.bfloat16)
    length, depth = own.shape
    height = length // (owned * sub)
    halves = 2 if height % 256 == 0 else 1

    def pieces(k):
        return halves if k else 1

    cols = [own]
    for t in range(1, sub):
        cols.append(lax.ppermute(own, "sub", [((u + t) % sub, u) for u in range(sub)]))
    views = [c.reshape(owned * sub, height, depth) for c in cols]

    places = [(a, b, c) for a in range(aux) for b in range(orb) for c in range(sub)]
    table = [[] for _ in places]

    def scalars(rows):
        at = len(table[0])
        for line_, row in zip(table, rows):
            line_.extend(int(value) for value in row)
        return at

    def own_block(a, b, c, q):
        return line.order(0, b, a)[q] % owned * sub + c

    events, finals = [], []
    for k in range(orb):
        base = (owned * k - 1 if k else 0) * halves
        wide = halves // pieces(k)
        ready = [base + q * halves - 0.4 if k else 0.25 * q - 1 for q in range(owned)]
        for q in range(owned):
            if k:
                events.append((-1.1 if q == 0 and k == 1 else -0.7, 0, "rows", k, q, 0))
            events.append((ready[q], 0, "product", k, q, 0))
        for group in line.merged(k):
            step = group[0][1]
            for c in range(pieces(k)):
                when = max(base + rank * halves + (c + st) * wide for rank, st in group)
                if step == 0 and c == 0:
                    when = ready[group[0][0]] + 0.1
                if not k and len(group) > 1:
                    when += 0.5
                events.append((when, step, "hop", k, tuple(group), c))
            if any(line.hop(k, *member)[2] for member in group):
                finals.append((k, tuple(group)))
    end = max(e[0] for e in events)
    for c in range(halves):
        events.append((end + 1, c, "fold", orb - 1, c, 0))
    events.sort(key=lambda e: e[:2])

    plans = []
    for _, _, kind, k, what, c in events:
        piece = height // pieces(k)
        plan = dict(kind=kind, k=k, what=what, c=c)
        if kind == "rows":
            rows = [[line.order(k, (b - k) % orb, a)[what] % owned * sub + d] for a, b, d in places]
        elif kind == "product":
            rows = [[t if k else own_block(a, b, d, what) for t in range(sub)] for a, b, d in places]
        elif kind == "hop":
            pairs, choices, tables = [], [], []
            for rank, step in what:
                more, position, _ = line.hop(k, rank, step)
                pairs += more
                for q in sorted(set(position.values())):
                    choices.append((rank, step, q))
                    tables.append([position.get(a * orb + b) == q for a, b, _ in places])
            plan.update(pairs=pairs, choices=choices)
            rows = []
            for i, (a, b, d) in enumerate(places):
                chosen = [t[i] for t in tables]
                start = sum(own_block(a, b, d, q) for (_, _, q), flag in zip(choices, chosen) if flag)
                rows.append(chosen + [start * height])
        else:
            piece = height // halves
            groups = [[group for k_, group in finals if k_ == phase] for phase in range(orb)]
            plan.update(groups=groups)
            rows = []
            for a, b, d in places:
                row = []
                for phase in range(orb):
                    row.append(a in line.targets(phase, b))
                    for group in groups[phase]:
                        row.append(any(a * orb + b in line.hop(phase, *member)[2] for member in group))
                rows.append(row + [(a % owned * sub + d) * height + what * piece])
        plan.update(at=scalars(rows), piece=piece)
        plans.append(plan)
    everywhere = lookup(table, place * sub + s)

    came_rows, sums, heads, came, result, last = {}, {}, {}, {}, None, None
    for plan in plans:
        k, what, c, at, piece = (plan[name] for name in ("k", "what", "c", "at", "piece"))
        extra = 0 if k else EXTRA
        if plan["kind"] == "rows":
            last = collect(after(everywhere, last), at, views)
            pairs = [((b + k) % orb, b) for b in range(orb)]
            came_rows[k, what] = lax.ppermute(last, "orb", pairs)
        elif plan["kind"] == "product":
            rows = [came_rows[k, what]] * sub if k else views
            flops = 2 * sub * height * length * depth if k and what == 0 else COST
            sums[k, what], *heads[k, what] = row_product(
                after(everywhere, last),
                at,
                rows,
                cols,
                pieces(k),
                extra,
                flops,
            )
            last = sums[k, what]
        elif plan["kind"] == "hop":
            choices = plan["choices"]
            if choices[0][1] == 0:
                value = heads[k, choices[0][2]][c]
                for i, (_, _, q) in enumerate(choices[1:]):
                    value = jnp.where(everywhere[at + 1 + i] > 0, heads[k, q][c], value)
                value = after(value, last) if c or len(choices) > 1 else value
            else:
                value = forward(
                    after(everywhere, last),
                    at,
                    [sums[k, q] for _, _, q in choices],
                    [came[k, rank, step - 1, c] for rank, step, _ in choices],
                    piece,
                    c,
                    FORWARD_COST if k and c == 0 and choices[0][:2] == (0, 1) else COST,
                )
            last = value
            arrived = lax.ppermute(value, ("aux", "orb"), plan["pairs"])
            for member in what:
                came[(k,) + member + (c,)] = arrived
        else:
            phases = []
            for phase, groups in enumerate(plan["groups"]):
                part = what if pieces(phase) == halves else 0
                phases.append((sums[phase, owned - 1], [came[(phase,) + g[0] + (part,)] for g in groups]))
            result = fold(after(everywhere, last), at, phases, result, piece, what)
            last = result
    return result


def solution(mesh):
    return jax.shard_map(
        functools.partial(shards, mesh),
        mesh=mesh,
        in_specs=(
            P(("groups", "aux"), "orb", None, None, None),
            P(("groups", "aux"), "orb", None),
            P(("groups", "aux"), "orb"),
            P(("groups", "orb"), "sub"),
        ),
        out_specs=P(("groups", "aux", "sub"), "orb"),
        check_vma=False,
    )
```
